512 devices in a mesh: seq: 128 (over x, z, core), head: 4 (over y).
Axes of the slice: x: 4, y: 4, z: 16, core: 2. Of those that a mesh axis runs over, the one named last changes fastest.
Arguments:
- tile_rows: bfloat16 [65536, 512], P('seq', 'head'), as said below
- tile_order: int32 [65536], P('seq'), may hold values from 0 to 65535, as said below
- tissue_mask: int32 [65536], P('seq'), may hold values from 0 to 1, as said below
- conv_weight: bfloat16 [512, 64, 512], P('seq', None, 'head'), may hold values from -0.03125 to 0.03125
- conv_bias: float32 [512], P('head'), may hold values from -3 to 3
- norm_gain: float32 [512], P('head'), may hold values from 0.1 to 1.9
- norm_bias: float32 [512], P('head'), may hold values from -3 to 3
- query_weight: bfloat16 [512, 512], P(None, 'head'), may hold values from -0.796875 to 0.796875
- key_weight: bfloat16 [512, 512], P(None, 'head'), may hold values from -0.25 to 0.25
- value_weight: bfloat16 [512, 512], P(None, 'head'), may hold values from -0.25 to 0.25
- out_weight: bfloat16 [512, 512], P('head'), may hold values from -0.25 to 0.25
Outputs:
- attention_out: bfloat16 [65536, 512], P('seq', 'head')
The draws below stay inside these ranges and needn't reach their ends.
Inputs may be any that keep to these rules, and one draw needn't show every extreme that they name: `tile_rows`: features of the tiles. `tile_order`: A permutation of the grid positions. Grid blocks of 8 x 8 tiles are numbered row-major and owned in runs of 8 by the indices of seq in order; of the 512 tiles of one index of seq, at most 8 lie in the blocks of one owner, and every index of seq has 8 in the blocks of some owner. `tissue_mask`: 1 marks tissue, 0 background.
All inputs are finite; a program needn't handle non-finite values.
Results may differ from the reference program's by a relative error of at most 0.015.
The reference program's roundings to bfloat16 on the way count: a program that leaves them out, or rounds other values in their place, can miss the bound.
Values may be sent and summed in bfloat16 or wider, within the bound.
No kernel may reach another device: no remote copies, remote signals or barrier semaphores. Data moves between devices by JAX's collectives and lax.ppermute only.
A program may use at most 64 MiB of HBM per device.

```python
import math
import jax
import jax.numpy as jnp
from jax import lax

WIDTH = 512
HEADS = 8
HEAD_SIZE = 64
REDUCE = 8
GRID_W = 512
TOK_DEV = 512
TOKENS = 65536
GRID_H = 128
PATCH = 64
KEYS = 1024
BLK_DEV = 8
N_SEQ = 128
N_HEAD = 4


def draw_tile_rows(key, part):
    key = jax.random.fold_in(key, 37)
    first = jax.random.fold_in(key, 0)
    base = jax.random.normal(first, (TOKENS, WIDTH), jnp.float32)
    values = jnp.clip(base, -6.0, 6.0)
    return values.astype(jnp.bfloat16)


def draw_tile_order(key, part):
    key = jax.random.fold_in(key, 11)
    first, second, third, fourth = jax.random.split(key, 4)
    middle = TOK_DEV // N_SEQ
    pairs = (N_SEQ - 2) // 2
    spread = jax.random.randint(first, (pairs,), 0, middle).astype(jnp.int32)
    paired = jnp.stack([middle + spread, middle - spread], 1).reshape(-1)
    counts = jnp.concatenate([jnp.array([2 * middle, 0], jnp.int32), paired])
    counts = counts[jax.random.permutation(second, N_SEQ)]
    bounds = jnp.cumsum(counts)
    local = jnp.arange(TOK_DEV, dtype=jnp.int32)
    segment = jnp.sum((local[:, None] >= bounds[None, :]).astype(jnp.int32), 1)
    source = jnp.arange(N_SEQ, dtype=jnp.int32)
    owner = (source[:, None] + segment[None, :]) % N_SEQ
    owner_perm = jax.vmap(lambda sub: jax.random.permutation(sub, TOK_DEV))(jax.random.split(third, N_SEQ)).astype(jnp.int32)
    slots = owner_perm[owner, jnp.broadcast_to(local[None, :], owner.shape)]
    block = owner * BLK_DEV + slots // PATCH
    offset = slots % PATCH
    per_row = GRID_W // REDUCE
    grid_row = block // per_row * REDUCE + offset // REDUCE
    grid_col = block % per_row * REDUCE + offset % REDUCE
    position = grid_row * GRID_W + grid_col
    shuffle = jax.vmap(lambda sub: jax.random.permutation(sub, TOK_DEV))(jax.random.split(fourth, N_SEQ)).astype(jnp.int32)
    ordered = jnp.take_along_axis(position, shuffle, 1)
    return ordered.reshape(-1).astype(jnp.int32)


def draw_tissue_mask(key, part):
    key = jax.random.fold_in(key, 23)
    position = jnp.arange(TOKENS, dtype=jnp.int32)
    limit = 950 - 900 * position // TOKENS
    rolled = jax.random.randint(key, (TOKENS,), 0, 1000)
    return (rolled < limit).astype(jnp.int32)


def block_levels(own_key, dims, cuts, low, largest):
    factor_of, own = 1.0, jax.random.fold_in(own_key, 6)
    for dim, blocks in cuts:
        steps = jnp.exp(jax.random.uniform(jax.random.fold_in(own, dim), (blocks,), jnp.float32, low / len(cuts), largest / len(cuts)))
        factor_of = factor_of * jnp.repeat(steps, dims[dim] // blocks).reshape([-1 if axis == dim else 1 for axis in range(len(dims))])
    return factor_of


def normal_values(rng, shape, scale, bound, cuts=(), kind=jnp.bfloat16):
    values = scale * jax.random.normal(rng, shape, jnp.float32)
    if cuts:
        values = values * block_levels(rng, shape, cuts, -0.22, 0.18)
    return jnp.clip(values, -bound, bound).astype(kind)


def setup_inputs(seed: int = 0) -> dict:
    seeds = jax.random.split(jax.random.key(seed), 12)
    return {
        "tile_rows": draw_tile_rows(jax.random.fold_in(seeds[11], 71), 0),
        "tile_order": draw_tile_order(jax.random.fold_in(seeds[11], 71), 0),
        "tissue_mask": draw_tissue_mask(jax.random.fold_in(seeds[11], 71), 0),
        "conv_weight": normal_values(seeds[3], (WIDTH, PATCH, WIDTH), (PATCH * WIDTH) ** -0.5, 0.03125, ((0, 128), (2, 4))),
        "conv_bias": normal_values(seeds[4], (WIDTH,), 0.5, 3.0, ((0, 4),), jnp.float32),
        "norm_gain": jnp.clip(1.0 + 0.18 * jax.random.normal(seeds[5], (WIDTH,), jnp.float32), 0.1, 1.9),
        "norm_bias": normal_values(seeds[6], (WIDTH,), 0.5, 3.0, ((0, 4),), jnp.float32),
        "query_weight": normal_values(seeds[7], (WIDTH, WIDTH), 0.1326, 0.796875, ((1, 4),)),
        "key_weight": normal_values(seeds[8], (WIDTH, WIDTH), WIDTH ** -0.5, 0.25, ((1, 4),)),
        "value_weight": normal_values(seeds[9], (WIDTH, WIDTH), WIDTH ** -0.5, 0.25, ((1, 4),)),
        "out_weight": normal_values(seeds[10], (WIDTH, WIDTH), WIDTH ** -0.5, 0.25, ((0, 4),)),
    }


def reference(tile_rows, tile_order, tissue_mask, conv_weight, conv_bias, norm_gain, norm_bias, query_weight, key_weight, value_weight, out_weight):
    flags = tissue_mask.astype(jnp.bfloat16)
    masked = tile_rows * flags[:, None]
    grid = jnp.zeros((TOKENS, WIDTH), jnp.bfloat16).at[tile_order].set(masked)
    per_row = GRID_W // REDUCE
    grid = grid.reshape(GRID_H // REDUCE, REDUCE, per_row, REDUCE, WIDTH)
    patches = grid.transpose(0, 2, 1, 3, 4).reshape(KEYS, PATCH * WIDTH)
    kernel = conv_weight.reshape(WIDTH, PATCH * WIDTH).T
    reduced = jnp.dot(patches, kernel, preferred_element_type=jnp.float32) + conv_bias[None, :]
    center = lax.optimization_barrier(jnp.mean(reduced, 1, keepdims=True))
    second = lax.optimization_barrier(jnp.mean(reduced * reduced, 1, keepdims=True))
    normed = ((reduced - center) * lax.rsqrt(second - center * center + 1e-05) * norm_gain + norm_bias).astype(jnp.bfloat16)
    keys = jnp.dot(normed, key_weight, preferred_element_type=jnp.float32).astype(jnp.bfloat16)
    values = jnp.dot(normed, value_weight, preferred_element_type=jnp.float32).astype(jnp.bfloat16)
    queries = jnp.dot(tile_rows, query_weight, preferred_element_type=jnp.float32).astype(jnp.bfloat16)
    scale = 1.0 / math.sqrt(HEAD_SIZE)
    keys3 = keys.astype(jnp.float32).reshape(KEYS, HEADS, HEAD_SIZE)
    values3 = values.astype(jnp.float32).reshape(KEYS, HEADS, HEAD_SIZE)

    def attend(query_block):
        query3 = query_block.astype(jnp.float32).reshape(-1, HEADS, HEAD_SIZE)
        scores = jnp.einsum('thd,khd->htk', query3, keys3) * scale
        highest = lax.optimization_barrier(jnp.max(scores, -1, keepdims=True))
        weights = jnp.exp(scores - highest)
        totals = lax.optimization_barrier(jnp.sum(weights, -1))
        probs = weights.astype(jnp.bfloat16).astype(jnp.float32)
        mixed = jnp.einsum('htk,khd->thd', probs, values3) / totals.T[:, :, None]
        return mixed.reshape(-1, WIDTH).astype(jnp.bfloat16)
    attended = lax.map(attend, queries.reshape(-1, 1024, WIDTH)).reshape(TOKENS, WIDTH)
    group = WIDTH // N_HEAD
    summed = jnp.zeros((TOKENS, WIDTH), jnp.float32)
    for index in range(N_HEAD):
        part = jnp.dot(attended[:, index * group:(index + 1) * group], out_weight[index * group:(index + 1) * group], preferred_element_type=jnp.float32).astype(jnp.bfloat16)
        summed = summed + part.astype(jnp.float32)
    return (summed * tissue_mask[:, None].astype(jnp.float32)).astype(jnp.bfloat16)
```

```python
import math

import jax
import jax.numpy as jnp
from jax import lax
from jax.experimental import pallas as pl
from jax.experimental.pallas import tpu as pltpu
from jax.sharding import Mesh
from jax.sharding import PartitionSpec as P

NX, NZ, NC, NH = 4, 16, 2, 4
PLANE = NX * NC
SLOTS = 8
ROWS = PLANE * SLOTS
SEND = ROWS + 16
TOK = 512
LANES = 128
BLK = 8
PATCH = 64
EMPTY = 1024.0
F32 = jnp.float32
BF16 = jnp.bfloat16
NT = (((1,), (1,)), ((), ()))


def params(mib):
    return pltpu.CompilerParams(vmem_limit_bytes=mib * 1024 * 1024)


def iota(shape, dim):
    return lax.broadcasted_iota(jnp.int32, shape, dim)


def route_kernel(rows_ref, order_ref, mask_ref, out_ref):
    order = order_ref[...]
    row, col = order >> 9, order & 511
    owner = (row >> 3) * 8 + (col >> 6)
    plane = (owner >> 1) & 15
    place = (owner >> 5) * 2 + (owner & 1)
    target = ((row & 7) * 8 + (col & 7)) * BLK + ((col >> 3) & 7)
    code = plane * PLANE + place
    onehot = jnp.where(iota((128, TOK), 0) == code, 1.0, 0.0)
    before = jnp.where(iota((TOK, TOK), 0) < iota((TOK, TOK), 1), 1.0, 0.0).astype(BF16)
    counts = jnp.dot(onehot.astype(BF16), before, preferred_element_type=F32)
    rank = jnp.sum(onehot * counts, 0, keepdims=True).astype(jnp.int32)
    slot = place * SLOTS + rank
    here = iota((NZ, TOK), 0) == plane
    value = jnp.where(here, (target - 256).astype(F32), 0.0).astype(BF16)
    there = jnp.where(here, 1.0, 0.0).astype(BF16)
    lane_of = jnp.where(iota((LANES, TOK), 0) == slot, 1.0, 0.0).astype(BF16)
    values = lax.dot_general(value, lane_of, NT, preferred_element_type=F32)
    valid = lax.dot_general(there, lane_of, NT, preferred_element_type=F32)
    meta = jnp.where(valid > 0.5, values, EMPTY)
    wanted = jnp.where(mask_ref[...] != 0, plane * ROWS + slot, -1)
    rows = rows_ref[...]
    for z in range(NZ):
        pick = jnp.where(iota((ROWS, TOK), 0) + z * ROWS == wanted, 1.0, 0.0).astype(BF16)
        out_ref[z, 0:ROWS, :] = jnp.dot(pick, rows, preferred_element_type=F32).astype(BF16)
        out_ref[z, ROWS:SEND, :] = jnp.broadcast_to(meta[z : z + 1, :], (16, LANES)).astype(BF16)


def conv_kernel(near_ref, far_ref, weight_ref, param_ref, out_ref, patch_ref):
    spot = (iota((TOK, LANES), 0) - 256).astype(F32)
    for owner in range(PLANE):
        total = None
        for ref in (near_ref, far_ref):
            for x in range(NX):
                meta = ref[x, PLANE * 128 : PLANE * 128 + 16, :].astype(F32)[owner : owner + 1, :]
                pick = jnp.where(spot == meta, 1.0, 0.0).astype(BF16)
                part = jnp.dot(
                    pick,
                    ref[x, owner * 128 : owner * 128 + 128, :],
                    preferred_element_type=F32,
                )
                total = part if total is None else total + part
        patch_ref[:, owner * BLK : owner * BLK + BLK, :] = total.reshape(PATCH, BLK, LANES)
    acc = jnp.zeros((256, 256), F32)
    for quad in range(16):
        left = weight_ref[:, quad * 16 : quad * 16 + 16, :].reshape(256, LANES)
        right = patch_ref[quad * 4 : quad * 4 + 4, :, :].astype(BF16).reshape(256, LANES)
        acc = acc + lax.dot_general(right, left, NT, preferred_element_type=F32)
    column = iota((64, 256), 1)
    kept = jnp.zeros((64, 256), F32)
    for step in range(4):
        kept = kept + jnp.where(
            ((column >> 2) & 3) == step, acc[step * 64 : step * 64 + 64, :], 0.0
        )
    source, lane = iota((256, LANES), 0), iota((256, LANES), 1)
    merge = jnp.where(((source >> 4) * 4 + (source & 3)) == lane, 1.0, 0.0)
    sums = jnp.dot(
        kept, merge, precision=lax.Precision.HIGHEST, preferred_element_type=F32
    )
    sent = sums.reshape(PLANE, BLK, LANES) + param_ref[...][None]
    for head in range(NH):
        out_ref[:, head] = sent


def norm_kernel(sums_ref, key_ref, value_ref, out_ref):
    left = iota((BLK, LANES), 1) < 64
    shares, gains, biases = [], [], []
    for x in range(NX):
        for c in range(NC):
            total = sums_ref[x, c, 0]
            for head in range(1, NH):
                total = total + sums_ref[x, c, head]
            extra = pltpu.roll(sums_ref[x, c, x], 64, 1)
            gains.append(extra[c : c + 1, :])
            biases.append(extra[2 + c : 3 + c, :])
            shares.append(jnp.where(left, total + extra[4 + c : 5 + c, :], 0.0))
    first = shares[0]
    second = shares[0] * shares[0]
    for share in shares[1:]:
        first = first + share
        second = second + share * share
    center = jnp.sum(first, 1, keepdims=True) * (1.0 / 512)
    spread = jnp.sum(second, 1, keepdims=True) * (1.0 / 512)
    scale = lax.rsqrt(spread - center * center + 1e-05)
    keys = jnp.zeros((BLK, LANES), F32)
    values = jnp.zeros((BLK, LANES), F32)
    source, lane = iota((LANES, LANES), 0), iota((LANES, LANES), 1)
    for x in range(NX):
        spread_out = None
        for c in range(NC):
            index = x * NC + c
            normed = (shares[index] - center) * scale * gains[index] + biases[index]
            normed = jnp.where(left, normed, 0.0).astype(BF16)
            hit = (lane == (source >> 2) * 8 + c * 4 + (source & 3)) & (source < 64)
            part = jnp.dot(
                normed, jnp.where(hit, 1.0, 0.0).astype(BF16), preferred_element_type=F32
            )
            spread_out = part if spread_out is None else spread_out + part
        natural = spread_out.astype(BF16)
        keys = keys + jnp.dot(
            natural, key_ref[x * 128 : x * 128 + 128, :], preferred_element_type=F32
        )
        values = values + jnp.dot(
            natural, value_ref[x * 128 : x * 128 + 128, :], preferred_element_type=F32
        )
    both = jnp.concatenate([keys, values], 1).astype(BF16)
    for z in range(NZ):
        out_ref[z] = both


def query_kernel(features_ref, weight_ref, out_ref):
    total = None
    for head in range(NH):
        part = jnp.dot(
            features_ref[head],
            weight_ref[head * 128 : head * 128 + 128, :],
            preferred_element_type=F32,
        )
        total = part if total is None else total + part
    out_ref[...] = total.astype(BF16)


def attend_kernel(query_ref, key_value_ref, weight_ref, out_ref):
    factor = math.log2(math.e) / math.sqrt(64)
    step = 256
    keys = key_value_ref[:, 0:128]
    values = key_value_ref[:, 128:256]
    weight = weight_ref[...]
    lane = iota((step, LANES), 1)
    for start in range(0, TOK, step):
        query = query_ref[start : start + step, :]
        mixed = []
        for head in range(2):
            mine = (lane >> 6) == head
            masked = jnp.where(mine, query.astype(F32), 0.0).astype(BF16)
            scores = lax.dot_general(masked, keys, NT, preferred_element_type=F32)
            highest = jnp.max(scores, 1, keepdims=True)
            weights = jnp.exp2((scores - highest) * factor)
            totals = jnp.sum(weights, 1, keepdims=True)
            mix = jnp.dot(weights.astype(BF16), values, preferred_element_type=F32)
            mixed.append(mix / totals)
        attended = jnp.where(lane < 64, mixed[0], mixed[1]).astype(BF16)
        part = jnp.dot(attended, weight, preferred_element_type=F32).astype(BF16)
        for group in range(NH):
            out_ref[group, start : start + step, :] = part[:, group * 128 : group * 128 + 128]


def local(
    tile_rows,
    tile_order,
    tissue_mask,
    conv_weight,
    conv_bias,
    norm_gain,
    norm_bias,
    query_weight,
    key_weight,
    value_weight,
    out_weight,
):
    shape = jax.ShapeDtypeStruct
    turned = conv_weight.transpose(1, 0, 2).reshape(256, LANES)
    weights = lax.all_gather(turned, "z", axis=0, tiled=True).reshape(NZ, 256, LANES)
    sorted_rows = pl.pallas_call(
        route_kernel,
        out_shape=shape((NZ, SEND, LANES), BF16),
        compiler_params=params(32),
    )(tile_rows, tile_order.reshape(1, TOK), tissue_mask.reshape(1, TOK))
    arrived = lax.all_to_all(sorted_rows, "z", split_axis=0, concat_axis=0, tiled=True)
    payload = arrived[:, :ROWS].reshape(NZ, PLANE, SLOTS, LANES).transpose(1, 0, 2, 3)
    places = arrived[:, ROWS, :ROWS].reshape(NZ, PLANE, SLOTS).transpose(1, 0, 2)
    places = jnp.pad(places.reshape(PLANE, LANES), ((0, 8), (0, 0)))
    here = jnp.concatenate([payload.reshape(PLANE * 128, LANES), places], 0)
    near = lax.all_to_all(
        jnp.broadcast_to(here[None], (NX,) + here.shape), "x", split_axis=0, concat_axis=0, tiled=True
    )
    far = lax.ppermute(near, "core", [(0, 1), (1, 0)])
    features = lax.all_gather(tile_rows, "head", axis=0)
    queries = pl.pallas_call(
        query_kernel, out_shape=shape((TOK, LANES), BF16), compiler_params=params(32)
    )(features, query_weight)
    extra = jnp.stack([norm_gain, norm_bias, conv_bias]).reshape(3, NZ, NC, 4)
    extra = jnp.pad(extra.transpose(0, 2, 1, 3).reshape(6, 64), ((0, 2), (64, 0)))
    partial = pl.pallas_call(
        conv_kernel,
        out_shape=shape((PLANE, NH, BLK, LANES), F32),
        scratch_shapes=[pltpu.VMEM((PATCH, 64, LANES), F32)],
        compiler_params=params(48),
    )(near, far, weights, extra)
    sums = lax.all_to_all(
        partial.reshape(PLANE * NH, BLK, LANES),
        ("x", "core", "head"),
        split_axis=0,
        concat_axis=0,
        tiled=True,
    )
    key_value = pl.pallas_call(
        norm_kernel, out_shape=shape((NZ, BLK, 256), BF16), compiler_params=params(32)
    )(sums.reshape(NX, NC, NH, BLK, LANES), key_weight, value_weight)
    gathered = lax.all_to_all(key_value, "z", split_axis=0, concat_axis=0, tiled=True)
    gathered = gathered.reshape(NZ * BLK, 256)
    gathered = lax.all_gather(gathered, "x", axis=0, tiled=True)
    gathered = lax.all_gather(gathered, "core", axis=0, tiled=True)
    parts = pl.pallas_call(
        attend_kernel, out_shape=shape((NH, TOK, LANES), BF16), compiler_params=params(48)
    )(queries, gathered, out_weight)
    parts = lax.all_to_all(parts, "head", split_axis=0, concat_axis=0, tiled=True)
    summed = jnp.sum(parts.astype(F32), 0)
    return (summed * tissue_mask[:, None].astype(F32)).astype(BF16)


def solution(mesh):
    grid = Mesh(mesh.devices.reshape(NX, NZ, NC, NH), ("x", "z", "core", "head"))
    seq = ("x", "z", "core")
    return jax.shard_map(
        local,
        mesh=grid,
        in_specs=(
            P(seq, "head"),
            P(seq),
            P(seq),
            P(seq, None, "head"),
            P("head"),
            P("head"),
            P("head"),
            P(None, "head"),
            P(None, "head"),
            P(None, "head"),
            P("head", None),
        ),
        out_specs=P(seq, "head"),
        check_vma=False,
    )
```

```python
import math

import jax
import jax.numpy as jnp
from jax import lax
from jax.experimental import pallas as pl
from jax.experimental.pallas import tpu as pltpu
from jax.sharding import Mesh
from jax.sharding import PartitionSpec as P

NX, NZ, NC, NH = 4, 16, 2, 4
PLANE = NX * NC
SLOTS = 8
ROWS = PLANE * SLOTS
SEND = ROWS + 32
TOK = 512
MOST = 240
WIDE = TOK + 48
LANES = 128
BLK = 8
PATCH = 64
EMPTY = 1024.0
F32 = jnp.float32
BF16 = jnp.bfloat16
NT = (((1,), (1,)), ((), ()))


def params(mib):
    return pltpu.CompilerParams(vmem_limit_bytes=mib * 1024 * 1024)


def iota(shape, dim):
    return lax.broadcasted_iota(jnp.int32, shape, dim)


def route_kernel(rows_ref, order_ref, mask_ref, tail_ref, gain_ref, shift_ref, bias_ref, out_ref, wide_ref):
    wide_ref[0:TOK, :] = rows_ref[...]
    whole = jnp.concatenate(
        [gain_ref[...], shift_ref[...], bias_ref[...], jnp.zeros((13, LANES), F32)], 0
    )
    high = whole.astype(BF16)
    rest = whole - high.astype(F32)
    middle = rest.astype(BF16)
    low = (rest - middle.astype(F32)).astype(BF16)
    wide_ref[TOK : TOK + 16, :] = high
    wide_ref[TOK + 16 : TOK + 32, :] = middle
    wide_ref[TOK + 32 : WIDE, :] = low
    order = order_ref[...]
    row, col = order >> 9, order & 511
    owner = (row >> 3) * 8 + (col >> 6)
    plane = (owner >> 1) & 15
    place = (owner >> 5) * 2 + (owner & 1)
    target = ((row & 7) * 8 + (col & 7)) * BLK + ((col >> 3) & 7)
    code = plane * PLANE + place
    onehot = jnp.where(iota((128, TOK), 0) == code, 1.0, 0.0)
    before = jnp.where(iota((TOK, TOK), 0) < iota((TOK, TOK), 1), 1.0, 0.0).astype(BF16)
    counts = jnp.dot(onehot.astype(BF16), before, preferred_element_type=F32)
    rank = jnp.sum(onehot * counts, 0, keepdims=True).astype(jnp.int32)
    slot = place * SLOTS + rank
    here = iota((NZ, TOK), 0) == plane
    value = jnp.where(here, (target - 256).astype(F32), 0.0).astype(BF16)
    there = jnp.where(here, 1.0, 0.0).astype(BF16)
    lane_of = jnp.where(iota((LANES, TOK), 0) == slot, 1.0, 0.0).astype(BF16)
    values = lax.dot_general(value, lane_of, NT, preferred_element_type=F32)
    valid = lax.dot_general(there, lane_of, NT, preferred_element_type=F32)
    meta = jnp.where(valid > 0.5, values, EMPTY)
    wanted = jnp.where(mask_ref[...] != 0, plane * ROWS + slot, -1)
    rows = rows_ref[...]
    for z in range(NZ):
        pick = jnp.where(iota((ROWS, TOK), 0) + z * ROWS == wanted, 1.0, 0.0).astype(BF16)
        out_ref[z, 0:ROWS, :] = jnp.dot(pick, rows, preferred_element_type=F32).astype(BF16)
        out_ref[z, ROWS : ROWS + 16, :] = jnp.broadcast_to(meta[z : z + 1, :], (16, LANES)).astype(BF16)
        out_ref[z, ROWS + 16 : SEND, :] = tail_ref[...]


def place_kernel(near_ref, far_ref, out_ref, patch_ref):
    spot = (iota((TOK, LANES), 0) - 256).astype(F32)
    for owner in range(PLANE):
        total = None
        for ref in (near_ref, far_ref):
            for x in range(NX):
                meta = ref[x, PLANE * 128 : PLANE * 128 + 16, :].astype(F32)[owner : owner + 1, :]
                pick = jnp.where(spot == meta, 1.0, 0.0).astype(BF16)
                part = jnp.dot(
                    pick,
                    ref[x, owner * 128 : owner * 128 + 128, :],
                    preferred_element_type=F32,
                )
                total = part if total is None else total + part
        patch_ref[:, owner * BLK : owner * BLK + BLK, :] = total.reshape(PATCH, BLK, LANES)
    out_ref[...] = patch_ref[...].astype(BF16)


def conv_kernel(patch_ref, weight_ref, tail_ref, out_ref):
    acc = jnp.zeros((256, 256), F32)
    for quad in range(16):
        ref = weight_ref.at[:, quad * 16 : quad * 16 + 16, :] if quad < 15 else tail_ref
        left = ref[...].reshape(256, LANES)
        right = patch_ref[quad * 4 : quad * 4 + 4, :, :].reshape(256, LANES)
        acc = acc + lax.dot_general(right, left, NT, preferred_element_type=F32)
    column = iota((64, 256), 1)
    kept = jnp.zeros((64, 256), F32)
    for step in range(4):
        kept = kept + jnp.where(
            ((column >> 2) & 3) == step, acc[step * 64 : step * 64 + 64, :], 0.0
        )
    source, lane = iota((256, LANES), 0), iota((256, LANES), 1)
    from_lane = (source >> 4) * 4 + (source & 3)
    lower = jnp.where(from_lane == lane, 1.0, 0.0)
    upper = jnp.where(from_lane + 64 == lane, 1.0, 0.0)

    def merge(rows, hits):
        return jnp.dot(rows, hits, precision=lax.Precision.HIGHEST, preferred_element_type=F32)

    low = merge(kept, lower).reshape(NX, NC, BLK, LANES)
    high = merge(kept, upper).reshape(NX, NC, BLK, LANES)
    for c in range(NC):
        sent = (low[0:2, c] + high[2:4, c]).reshape(16, LANES)
        for x in range(NX):
            for head in range(NH):
                out_ref[x, c, head] = sent


def norm_kernel(sums_ref, wide_ref, key_ref, value_ref, out_ref):
    count = 32
    left = iota((count, LANES), 1) < 64
    source, lane = iota((LANES, LANES), 0), iota((LANES, LANES), 1)
    hits = [(lane == (source >> 2) * 8 + c * 4 + (source & 3)) & (source < 64) for c in range(NC)]
    backs = [(source == (lane >> 2) * 8 + c * 4 + (lane & 3)) & (lane < 64) for c in range(NC)]
    shares, gains, biases = [], [], []
    for x in range(NX):
        whole = (
            wide_ref[x, TOK : TOK + 16, :].astype(F32)
            + wide_ref[x, TOK + 16 : TOK + 32, :].astype(F32)
        ) + wide_ref[x, TOK + 32 : WIDE, :].astype(F32)
        for c in range(NC):
            total = sums_ref[x, c, 0]
            for head in range(1, NH):
                total = total + sums_ref[x, c, head]
            total = jnp.concatenate([total, pltpu.roll(total, 64, 1)], 0)
            extra = jnp.dot(
                whole,
                jnp.where(backs[c], 1.0, 0.0),
                precision=lax.Precision.HIGHEST,
                preferred_element_type=F32,
            )
            gains.append(extra[0:1, :])
            biases.append(extra[1:2, :])
            shares.append(jnp.where(left, total + extra[2:3, :], 0.0))
    first = shares[0]
    second = shares[0] * shares[0]
    for share in shares[1:]:
        first = first + share
        second = second + share * share
    center = jnp.sum(first, 1, keepdims=True) * (1.0 / 512)
    spread = jnp.sum(second, 1, keepdims=True) * (1.0 / 512)
    scale = lax.rsqrt(spread - center * center + 1e-05)
    keys = jnp.zeros((count, LANES), F32)
    values = jnp.zeros((count, LANES), F32)
    for x in range(NX):
        natural = None
        for c in range(NC):
            index = x * NC + c
            normed = (shares[index] - center) * scale * gains[index] + biases[index]
            normed = jnp.where(left, normed, 0.0).astype(BF16)
            part = jnp.dot(
                normed, jnp.where(hits[c], 1.0, 0.0).astype(BF16), preferred_element_type=F32
            )
            natural = part if natural is None else natural + part
        natural = natural.astype(BF16)
        keys = keys + jnp.dot(
            natural, key_ref[x * 128 : x * 128 + 128, :], preferred_element_type=F32
        )
        values = values + jnp.dot(
            natural, value_ref[x * 128 : x * 128 + 128, :], preferred_element_type=F32
        )
    both = jnp.concatenate([keys, values], 1).astype(BF16)
    for z in range(NZ):
        out_ref[z] = both


def query_kernel(features_ref, weight_ref, out_ref):
    total = None
    for head in range(NH):
        part = jnp.dot(
            features_ref[head, 0:TOK, :],
            weight_ref[head * 128 : head * 128 + 128, :],
            preferred_element_type=F32,
        )
        total = part if total is None else total + part
    out_ref[...] = total.astype(BF16)


def attend_kernel(query_ref, key_value_ref, weight_ref, out_ref):
    factor = math.log2(math.e) / math.sqrt(64)
    step = 256
    keys = key_value_ref[:, 0:128]
    values = key_value_ref[:, 128:256]
    weight = weight_ref[...]
    lane = iota((step, LANES), 1)
    for start in range(0, TOK, step):
        query = query_ref[start : start + step, :]
        mixed = []
        for head in range(2):
            mine = (lane >> 6) == head
            masked = jnp.where(mine, query.astype(F32), 0.0).astype(BF16)
            scores = lax.dot_general(masked, keys, NT, preferred_element_type=F32)
            highest = jnp.max(scores, 1, keepdims=True)
            weights = jnp.exp2((scores - highest) * factor)
            totals = jnp.sum(weights, 1, keepdims=True)
            mix = jnp.dot(weights.astype(BF16), values, preferred_element_type=F32)
            mixed.append(mix / totals)
        attended = jnp.where(lane < 64, mixed[0], mixed[1]).astype(BF16)
        part = jnp.dot(attended, weight, preferred_element_type=F32).astype(BF16)
        for group in range(NH):
            out_ref[group, start : start + step, :] = part[:, group * 128 : group * 128 + 128]


def local(
    tile_rows,
    tile_order,
    tissue_mask,
    conv_weight,
    conv_bias,
    norm_gain,
    norm_bias,
    query_weight,
    key_weight,
    value_weight,
    out_weight,
):
    shape = jax.ShapeDtypeStruct
    turned = conv_weight.transpose(1, 0, 2).reshape(256, LANES)
    sorted_rows, wide = pl.pallas_call(
        route_kernel,
        out_shape=(shape((NZ, SEND, LANES), BF16), shape((WIDE, LANES), BF16)),
        compiler_params=params(32),
    )(
        tile_rows,
        tile_order.reshape(1, TOK),
        tissue_mask.reshape(1, TOK),
        turned[MOST:],
        norm_gain.reshape(1, LANES),
        norm_bias.reshape(1, LANES),
        conv_bias.reshape(1, LANES),
    )
    arrived = lax.all_to_all(sorted_rows, "z", split_axis=0, concat_axis=0, tiled=True)
    features = lax.all_gather(wide, "head", axis=0)
    queries = pl.pallas_call(
        query_kernel, out_shape=shape((TOK, LANES), BF16), compiler_params=params(32)
    )(features, query_weight)
    arrived, most, queries = lax.optimization_barrier((arrived, turned[:MOST], queries))
    weights = lax.all_gather(most, "z", axis=0, tiled=True).reshape(NZ, MOST, LANES)
    payload = arrived[:, :ROWS].reshape(NZ, PLANE, SLOTS, LANES).transpose(1, 0, 2, 3)
    places = arrived[:, ROWS, :ROWS].reshape(NZ, PLANE, SLOTS).transpose(1, 0, 2)
    places = jnp.pad(places.reshape(PLANE, LANES), ((0, 8), (0, 0)))
    here = jnp.concatenate([payload.reshape(PLANE * 128, LANES), places], 0)
    near = lax.all_to_all(
        jnp.broadcast_to(here[None], (NX,) + here.shape), "x", split_axis=0, concat_axis=0, tiled=True
    )
    near, weights = lax.optimization_barrier((near, weights))
    far = lax.ppermute(near, "core", [(0, 1), (1, 0)])
    patches = pl.pallas_call(
        place_kernel,
        out_shape=shape((PATCH, 64, LANES), BF16),
        scratch_shapes=[pltpu.VMEM((PATCH, 64, LANES), F32)],
        compiler_params=params(48),
    )(near, far)
    partial = pl.pallas_call(
        conv_kernel,
        out_shape=shape((NX, NC, NH, 16, LANES), F32),
        compiler_params=params(48),
    )(patches, weights, arrived[:, ROWS + 16 :])
    sums = lax.all_to_all(
        partial.reshape(PLANE * NH, 16, LANES),
        ("x", "core", "head"),
        split_axis=0,
        concat_axis=0,
        tiled=True,
    )
    key_value = pl.pallas_call(
        norm_kernel, out_shape=shape((NZ, 32, 256), BF16), compiler_params=params(32)
    )(sums.reshape(NX, NC, NH, 16, LANES), features, key_weight, value_weight)
    gathered = lax.all_to_all(key_value, "z", split_axis=0, concat_axis=0, tiled=True)
    gathered = lax.all_gather(gathered.reshape(NZ * 32, 256), "core", axis=0, tiled=True)
    parts = pl.pallas_call(
        attend_kernel, out_shape=shape((NH, TOK, LANES), BF16), compiler_params=params(48)
    )(queries, gathered, out_weight)
    parts = lax.all_to_all(parts, "head", split_axis=0, concat_axis=0, tiled=True)
    summed = jnp.sum(parts.astype(F32), 0)
    return (summed * tissue_mask[:, None].astype(F32)).astype(BF16)


def solution(mesh):
    grid = Mesh(mesh.devices.reshape(NX, NZ, NC, NH), ("x", "z", "core", "head"))
    seq = ("x", "z", "core")
    return jax.shard_map(
        local,
        mesh=grid,
        in_specs=(
            P(seq, "head"),
            P(seq),
            P(seq),
            P(seq, None, "head"),
            P("head"),
            P("head"),
            P("head"),
            P(None, "head"),
            P(None, "head"),
            P(None, "head"),
            P("head", None),
        ),
        out_specs=P(seq, "head"),
        check_vma=False,
    )
```

```python
import math

import jax
import jax.numpy as jnp
from jax import lax
from jax.experimental import pallas as pl
from jax.experimental.pallas import tpu as pltpu
from jax.sharding import Mesh
from jax.sharding import PartitionSpec as P

NX, NZ, NC, NH = 4, 16, 2, 4
PLANE = NX * NC
SLOTS = 8
ROWS = PLANE * SLOTS
SEND = ROWS + 16
TOK = 512
MOST = 248
WIDE = TOK + 48
LANES = 128
BLK = 8
PATCH = 64
EMPTY = 1024.0
F32 = jnp.float32
BF16 = jnp.bfloat16
NT = (((1,), (1,)), ((), ()))


def params(mib):
    return pltpu.CompilerParams(vmem_limit_bytes=mib * 1024 * 1024)


def iota(shape, dim):
    return lax.broadcasted_iota(jnp.int32, shape, dim)


def route_kernel(
    rows_hbm, order_hbm, mask_hbm, kernel_hbm, gain_hbm, shift_hbm, bias_hbm,
    out_ref, wide_ref, most_ref,
    rows_ref, order_ref, mask_ref, kernel_ref, gain_ref, shift_ref, bias_ref, sems,
):
    pairs = (
        (order_hbm, order_ref),
        (mask_hbm, mask_ref),
        (rows_hbm, rows_ref),
        (kernel_hbm, kernel_ref),
        (gain_hbm, gain_ref),
        (shift_hbm, shift_ref),
        (bias_hbm, bias_ref),
    )
    copies = [
        pltpu.make_async_copy(source, held, sems.at[index])
        for index, (source, held) in enumerate(pairs)
    ]
    for copy in copies:
        copy.start()
    before = jnp.where(iota((TOK, TOK), 0) < iota((TOK, TOK), 1), 1.0, 0.0).astype(BF16)
    row256, lane256 = iota((256, 256), 0), iota((256, 256), 1)
    turn = jnp.where(lane256 == (row256 & 3) * PATCH + (row256 >> 2), 1.0, 0.0).astype(BF16)
    for copy in copies:
        copy.wait()
    wide_ref[0:TOK, :] = rows_ref[...]
    whole = jnp.concatenate(
        [gain_ref[...], shift_ref[...], bias_ref[...], jnp.zeros((13, LANES), F32)], 0
    )
    high = whole.astype(BF16)
    rest = whole - high.astype(F32)
    middle = rest.astype(BF16)
    low = (rest - middle.astype(F32)).astype(BF16)
    wide_ref[TOK : TOK + 16, :] = high
    wide_ref[TOK + 16 : TOK + 32, :] = middle
    wide_ref[TOK + 32 : WIDE, :] = low
    turned = jnp.dot(turn, kernel_ref[...], preferred_element_type=F32)
    most_ref[...] = turned[0:MOST, :].astype(BF16)
    tail = jnp.concatenate([turned[MOST:256, :], turned[MOST:256, :]], 0)
    order = order_ref[...]
    row, col = order >> 9, order & 511
    owner = (row >> 3) * 8 + (col >> 6)
    plane = (owner >> 1) & 15
    place = (owner >> 5) * 2 + (owner & 1)
    target = ((row & 7) * 8 + (col & 7)) * BLK + ((col >> 3) & 7)
    code = plane * PLANE + place
    onehot = jnp.where(iota((128, TOK), 0) == code, 1.0, 0.0)
    counts = jnp.dot(onehot.astype(BF16), before, preferred_element_type=F32)
    rank = jnp.sum(onehot * counts, 0, keepdims=True).astype(jnp.int32)
    slot = place * SLOTS + rank
    here = iota((NZ, TOK), 0) == plane
    value = jnp.where(here, (target - 256).astype(F32), 0.0).astype(BF16)
    there = jnp.where(here, 1.0, 0.0).astype(BF16)
    lane_of = jnp.where(iota((LANES, TOK), 0) == slot, 1.0, 0.0).astype(BF16)
    values = lax.dot_general(value, lane_of, NT, preferred_element_type=F32)
    valid = lax.dot_general(there, lane_of, NT, preferred_element_type=F32)
    meta = jnp.where(valid > 0.5, values, EMPTY)
    wanted = jnp.where(mask_ref[...] != 0, plane * ROWS + slot, -1)
    rows = rows_ref[...]
    top = iota((16, LANES), 0) < 8
    for z in range(NZ):
        pick = jnp.where(iota((ROWS, TOK), 0) + z * ROWS == wanted, 1.0, 0.0).astype(BF16)
        out_ref[z, 0:ROWS, :] = jnp.dot(pick, rows, preferred_element_type=F32).astype(BF16)
        last = jnp.where(top, jnp.broadcast_to(meta[z : z + 1, :], (16, LANES)), tail)
        out_ref[z, ROWS:SEND, :] = last.astype(BF16)


def conv_kernel(tile_ref, weight_ref, tail_ref, out_ref, patch_ref):
    spot = (iota((TOK, LANES), 0) - 256).astype(F32)
    metas = [
        tile_ref[x, c, PLANE * 128 : PLANE * 128 + 16, :].astype(F32)
        for x in range(NX)
        for c in range(NC)
    ]
    for owner in range(PLANE):
        total = None
        for x in range(NX):
            for c in range(NC):
                pick = jnp.where(spot == metas[x * NC + c][owner : owner + 1, :], 1.0, 0.0)
                part = jnp.dot(
                    pick.astype(BF16),
                    tile_ref[x, c, owner * 128 : owner * 128 + 128, :],
                    preferred_element_type=F32,
                )
                total = part if total is None else total + part
        patch_ref[:, owner * BLK : owner * BLK + BLK, :] = total.reshape(PATCH, BLK, LANES)
    acc = jnp.zeros((256, 256), F32)
    for quad in range(16):
        if quad < 15:
            left = weight_ref[:, quad * 16 : quad * 16 + 16, :]
        else:
            most = weight_ref[:, quad * 16 : MOST, :].astype(F32)
            left = jnp.concatenate([most, tail_ref[...].astype(F32)], 1).astype(BF16)
        left = left.reshape(256, LANES)
        right = patch_ref[quad * 4 : quad * 4 + 4, :, :].astype(BF16).reshape(256, LANES)
        acc = acc + lax.dot_general(right, left, NT, preferred_element_type=F32)
    column = iota((64, 256), 1)
    kept = jnp.zeros((64, 256), F32)
    for step in range(4):
        kept = kept + jnp.where(
            ((column >> 2) & 3) == step, acc[step * 64 : step * 64 + 64, :], 0.0
        )
    source, lane = iota((256, LANES), 0), iota((256, LANES), 1)
    from_lane = (source >> 4) * 4 + (source & 3)
    lower = jnp.where(from_lane == lane, 1.0, 0.0)
    upper = jnp.where(from_lane + 64 == lane, 1.0, 0.0)

    def merge(rows, hits):
        return jnp.dot(rows, hits, precision=lax.Precision.HIGHEST, preferred_element_type=F32)

    low = merge(kept, lower).reshape(NX, NC, BLK, LANES)
    high = merge(kept, upper).reshape(NX, NC, BLK, LANES)
    for c in range(NC):
        sent = (low[0:2, c] + high[2:4, c]).reshape(16, LANES)
        for x in range(NX):
            for head in range(NH):
                out_ref[x, c, head] = sent


def norm_kernel(sums_ref, wide_ref, key_ref, value_ref, out_ref):
    count = 32
    left = iota((count, LANES), 1) < 64
    source, lane = iota((LANES, LANES), 0), iota((LANES, LANES), 1)
    hits = [(lane == (source >> 2) * 8 + c * 4 + (source & 3)) & (source < 64) for c in range(NC)]
    backs = [(source == (lane >> 2) * 8 + c * 4 + (lane & 3)) & (lane < 64) for c in range(NC)]
    shares, gains, biases = [], [], []
    for x in range(NX):
        whole = (
            wide_ref[x, TOK : TOK + 16, :].astype(F32)
            + wide_ref[x, TOK + 16 : TOK + 32, :].astype(F32)
        ) + wide_ref[x, TOK + 32 : WIDE, :].astype(F32)
        for c in range(NC):
            total = sums_ref[x, c, 0]
            for head in range(1, NH):
                total = total + sums_ref[x, c, head]
            total = jnp.concatenate([total, pltpu.roll(total, 64, 1)], 0)
            extra = jnp.dot(
                whole,
                jnp.where(backs[c], 1.0, 0.0),
                precision=lax.Precision.HIGHEST,
                preferred_element_type=F32,
            )
            gains.append(extra[0:1, :])
            biases.append(extra[1:2, :])
            shares.append(jnp.where(left, total + extra[2:3, :], 0.0))
    first = shares[0]
    second = shares[0] * shares[0]
    for share in shares[1:]:
        first = first + share
        second = second + share * share
    center = jnp.sum(first, 1, keepdims=True) * (1.0 / 512)
    spread = jnp.sum(second, 1, keepdims=True) * (1.0 / 512)
    scale = lax.rsqrt(spread - center * center + 1e-05)
    keys = jnp.zeros((count, LANES), F32)
    values = jnp.zeros((count, LANES), F32)
    for x in range(NX):
        natural = None
        for c in range(NC):
            index = x * NC + c
            normed = (shares[index] - center) * scale * gains[index] + biases[index]
            normed = jnp.where(left, normed, 0.0).astype(BF16)
            part = jnp.dot(
                normed, jnp.where(hits[c], 1.0, 0.0).astype(BF16), preferred_element_type=F32
            )
            natural = part if natural is None else natural + part
        natural = natural.astype(BF16)
        keys = keys + jnp.dot(
            natural, key_ref[x * 128 : x * 128 + 128, :], preferred_element_type=F32
        )
        values = values + jnp.dot(
            natural, value_ref[x * 128 : x * 128 + 128, :], preferred_element_type=F32
        )
    both = jnp.concatenate([keys, values], 1).astype(BF16)
    for z in range(NZ):
        out_ref[z] = both


def query_kernel(features_ref, weight_ref, out_ref):
    total = None
    for head in range(NH):
        part = jnp.dot(
            features_ref[head, 0:TOK, :],
            weight_ref[head * 128 : head * 128 + 128, :],
            preferred_element_type=F32,
        )
        total = part if total is None else total + part
    out_ref[...] = total.astype(BF16)


def attend_kernel(query_ref, key_value_ref, weight_ref, out_ref):
    factor = math.log2(math.e) / math.sqrt(64)
    step = 256
    keys = key_value_ref[:, 0:128]
    values = key_value_ref[:, 128:256]
    weight = weight_ref[...]
    lane = iota((step, LANES), 1)
    for start in range(0, TOK, step):
        query = query_ref[start : start + step, :]
        mixed = []
        for head in range(2):
            mine = (lane >> 6) == head
            masked = jnp.where(mine, query.astype(F32), 0.0).astype(BF16)
            scores = lax.dot_general(masked, keys, NT, preferred_element_type=F32)
            highest = jnp.max(scores, 1, keepdims=True)
            weights = jnp.exp2((scores - highest) * factor)
            totals = jnp.sum(weights, 1, keepdims=True)
            mix = jnp.dot(weights.astype(BF16), values, preferred_element_type=F32)
            mixed.append(mix / totals)
        attended = jnp.where(lane < 64, mixed[0], mixed[1]).astype(BF16)
        part = jnp.dot(attended, weight, preferred_element_type=F32).astype(BF16)
        for group in range(NH):
            out_ref[group, start : start + step, :] = part[:, group * 128 : group * 128 + 128]


def local(
    tile_rows,
    tile_order,
    tissue_mask,
    conv_weight,
    conv_bias,
    norm_gain,
    norm_bias,
    query_weight,
    key_weight,
    value_weight,
    out_weight,
):
    shape = jax.ShapeDtypeStruct
    hbm = pl.BlockSpec(memory_space=pl.ANY)
    sorted_rows, wide, most = pl.pallas_call(
        route_kernel,
        out_shape=(
            shape((NZ, SEND, LANES), BF16),
            shape((WIDE, LANES), BF16),
            shape((MOST, LANES), BF16),
        ),
        in_specs=[hbm] * 7,
        scratch_shapes=[
            pltpu.VMEM((TOK, LANES), BF16),
            pltpu.VMEM((1, TOK), jnp.int32),
            pltpu.VMEM((1, TOK), jnp.int32),
            pltpu.VMEM((256, LANES), BF16),
            pltpu.VMEM((1, LANES), F32),
            pltpu.VMEM((1, LANES), F32),
            pltpu.VMEM((1, LANES), F32),
            pltpu.SemaphoreType.DMA((7,)),
        ],
        compiler_params=params(60),
    )(
        tile_rows,
        tile_order.reshape(1, TOK),
        tissue_mask.reshape(1, TOK),
        conv_weight.reshape(256, LANES),
        norm_gain.reshape(1, LANES),
        norm_bias.reshape(1, LANES),
        conv_bias.reshape(1, LANES),
    )
    arrived = lax.all_to_all(sorted_rows, "z", split_axis=0, concat_axis=0, tiled=True)
    features = lax.all_gather(wide, "head", axis=0)
    queries = pl.pallas_call(
        query_kernel, out_shape=shape((TOK, LANES), BF16), compiler_params=params(16)
    )(features, query_weight)
    arrived, most, queries = lax.optimization_barrier((arrived, most, queries))
    weights = lax.all_gather(most, "z", axis=0, tiled=True).reshape(NZ, MOST, LANES)
    both = lax.all_gather(arrived, "core", axis=0)
    payload = both[:, :, :ROWS].reshape(NC, NZ, PLANE, SLOTS, LANES).transpose(0, 2, 1, 3, 4)
    places = both[:, :, ROWS, :ROWS].reshape(NC, NZ, PLANE, SLOTS).transpose(0, 2, 1, 3)
    places = jnp.pad(places.reshape(NC, PLANE, LANES), ((0, 0), (0, 8), (0, 0)))
    here = jnp.concatenate([payload.reshape(NC, PLANE * 128, LANES), places], 1)
    tiles = lax.all_to_all(
        jnp.broadcast_to(here[None], (NX,) + here.shape), "x", split_axis=0, concat_axis=0, tiled=True
    )
    tail = arrived[:, ROWS + 8 :]
    partial = pl.pallas_call(
        conv_kernel,
        out_shape=shape((NX, NC, NH, 16, LANES), F32),
        scratch_shapes=[pltpu.VMEM((PATCH, 64, LANES), F32)],
        compiler_params=params(24),
    )(tiles, weights, tail)
    sums = lax.all_to_all(
        partial.reshape(PLANE * NH, 16, LANES),
        ("x", "core", "head"),
        split_axis=0,
        concat_axis=0,
        tiled=True,
    )
    key_value = pl.pallas_call(
        norm_kernel, out_shape=shape((NZ, 32, 256), BF16), compiler_params=params(16)
    )(sums.reshape(NX, NC, NH, 16, LANES), features, key_weight, value_weight)
    gathered = lax.all_to_all(key_value, "z", split_axis=0, concat_axis=0, tiled=True)
    gathered = lax.all_gather(gathered.reshape(NZ * 32, 256), "core", axis=0, tiled=True)
    parts = pl.pallas_call(
        attend_kernel, out_shape=shape((NH, TOK, LANES), BF16), compiler_params=params(24)
    )(queries, gathered, out_weight)
    parts = lax.all_to_all(parts, "head", split_axis=0, concat_axis=0, tiled=True)
    summed = jnp.sum(parts.astype(F32), 0)
    return (summed * tissue_mask[:, None].astype(F32)).astype(BF16)


def solution(mesh):
    grid = Mesh(mesh.devices.reshape(NX, NZ, NC, NH), ("x", "z", "core", "head"))
    seq = ("x", "z", "core")
    return jax.shard_map(
        local,
        mesh=grid,
        in_specs=(
            P(seq, "head"),
            P(seq),
            P(seq),
            P(seq, None, "head"),
            P("head"),
            P("head"),
            P("head"),
            P(None, "head"),
            P(None, "head"),
            P(None, "head"),
            P("head", None),
        ),
        out_specs=P(seq, "head"),
        check_vma=False,
    )
```

```python
import math

import jax
import jax.numpy as jnp
from jax import lax
from jax.experimental import pallas as pl
from jax.experimental.pallas import tpu as pltpu
from jax.sharding import Mesh
from jax.sharding import PartitionSpec as P

NX, NZ, NC, NH = 4, 16, 2, 4
PLANE = NX * NC
SLOTS = 8
ROWS = PLANE * SLOTS
SEND = ROWS + 16
TOK = 512
MOST = 248
WIDE = TOK + 48
LANES = 128
BLK = 8
PATCH = 64
EMPTY = 1024.0
F32 = jnp.float32
BF16 = jnp.bfloat16
NT = (((1,), (1,)), ((), ()))
TN = (((0,), (0,)), ((), ()))


def params(mib):
    return pltpu.CompilerParams(vmem_limit_bytes=mib * 1024 * 1024)


def iota(shape, dim):
    return lax.broadcasted_iota(jnp.int32, shape, dim)


def route_kernel(
    rows_hbm, order_hbm, mask_hbm, kernel_hbm, gain_hbm, shift_hbm, bias_hbm,
    out_ref, wide_ref, most_ref,
    rows_ref, order_ref, mask_ref, kernel_ref, gain_ref, shift_ref, bias_ref, sems,
):
    pairs = (
        (order_hbm, order_ref),
        (mask_hbm, mask_ref),
        (rows_hbm, rows_ref),
        (kernel_hbm, kernel_ref),
        (gain_hbm, gain_ref),
        (shift_hbm, shift_ref),
        (bias_hbm, bias_ref),
    )
    copies = [
        pltpu.make_async_copy(source, held, sems.at[index])
        for index, (source, held) in enumerate(pairs)
    ]
    for copy in copies:
        copy.start()
    before = jnp.where(iota((TOK, TOK), 0) < iota((TOK, TOK), 1), 1.0, 0.0).astype(BF16)
    row256, lane256 = iota((256, 256), 0), iota((256, 256), 1)
    turn = jnp.where(lane256 == (row256 & 3) * PATCH + (row256 >> 2), 1.0, 0.0).astype(BF16)
    for copy in copies:
        copy.wait()
    wide_ref[0:TOK, :] = rows_ref[...]
    whole = jnp.concatenate(
        [gain_ref[...], shift_ref[...], bias_ref[...], jnp.zeros((13, LANES), F32)], 0
    )
    high = whole.astype(BF16)
    rest = whole - high.astype(F32)
    middle = rest.astype(BF16)
    low = (rest - middle.astype(F32)).astype(BF16)
    wide_ref[TOK : TOK + 16, :] = high
    wide_ref[TOK + 16 : TOK + 32, :] = middle
    wide_ref[TOK + 32 : WIDE, :] = low
    turned = jnp.dot(turn, kernel_ref[...], preferred_element_type=F32)
    most_ref[...] = turned[0:MOST, :].astype(BF16)
    tail = jnp.concatenate([turned[MOST:256, :], turned[MOST:256, :]], 0)
    order = order_ref[...]
    row, col = order >> 9, order & 511
    owner = (row >> 3) * 8 + (col >> 6)
    plane = (owner >> 1) & 15
    place = (owner >> 5) * 2 + (owner & 1)
    target = ((row & 7) * 8 + (col & 7)) * BLK + ((col >> 3) & 7)
    code = plane * PLANE + place
    onehot = jnp.where(iota((128, TOK), 0) == code, 1.0, 0.0)
    counts = jnp.dot(onehot.astype(BF16), before, preferred_element_type=F32)
    rank = jnp.sum(onehot * counts, 0, keepdims=True).astype(jnp.int32)
    slot = place * SLOTS + rank
    here = iota((NZ, TOK), 0) == plane
    value = jnp.where(here, (target - 256).astype(F32), 0.0).astype(BF16)
    there = jnp.where(here, 1.0, 0.0).astype(BF16)
    lane_of = jnp.where(iota((LANES, TOK), 0) == slot, 1.0, 0.0).astype(BF16)
    values = lax.dot_general(value, lane_of, NT, preferred_element_type=F32)
    valid = lax.dot_general(there, lane_of, NT, preferred_element_type=F32)
    meta = jnp.where(valid > 0.5, values, EMPTY)
    wanted = jnp.where(mask_ref[...] != 0, plane * ROWS + slot, -1)
    rows = rows_ref[...]
    top = iota((16, LANES), 0) < 8
    for z in range(NZ):
        pick = jnp.where(iota((ROWS, TOK), 0) + z * ROWS == wanted, 1.0, 0.0).astype(BF16)
        out_ref[z, 0:ROWS, :] = jnp.dot(pick, rows, preferred_element_type=F32).astype(BF16)
        last = jnp.where(top, jnp.broadcast_to(meta[z : z + 1, :], (16, LANES)), tail)
        out_ref[z, ROWS:SEND, :] = last.astype(BF16)


def place_kernel(tile_ref, out_ref, patch_ref):
    spot = (iota((TOK, LANES), 0) - 256).astype(F32)
    metas = [
        tile_ref[x, c, PLANE * 128 : PLANE * 128 + 16, :].astype(F32)
        for x in range(NX)
        for c in range(NC)
    ]
    for owner in range(PLANE):
        picks, tiles = [], []
        for x in range(NX):
            for c in range(NC):
                meta = metas[x * NC + c][owner : owner + 1, :]
                picks.append(jnp.where(spot == meta, 1.0, 0.0).astype(BF16))
                tiles.append(tile_ref[x, c, owner * 128 : owner * 128 + 128, :])
        total = jnp.dot(
            jnp.concatenate(picks, 1), jnp.concatenate(tiles, 0), preferred_element_type=F32
        )
        patch_ref[:, owner * BLK : owner * BLK + BLK, :] = total.reshape(PATCH, BLK, LANES)
    out_ref[...] = patch_ref[...].astype(BF16)


def conv_kernel(patch_ref, weight_ref, tail_ref, out_ref):
    acc = jnp.zeros((256, 256), F32)
    for quad in range(16):
        if quad < 15:
            left = weight_ref[:, quad * 16 : quad * 16 + 16, :]
        else:
            most = weight_ref[:, quad * 16 : MOST, :].astype(F32)
            left = jnp.concatenate([most, tail_ref[...].astype(F32)], 1).astype(BF16)
        left = left.reshape(256, LANES)
        right = patch_ref[quad * 4 : quad * 4 + 4, :, :].reshape(256, LANES)
        acc = acc + lax.dot_general(right, left, NT, preferred_element_type=F32)
    column = iota((64, 256), 1)
    kept = jnp.zeros((64, 256), F32)
    for step in range(4):
        kept = kept + jnp.where(
            ((column >> 2) & 3) == step, acc[step * 64 : step * 64 + 64, :], 0.0
        )
    source, lane = iota((256, LANES), 0), iota((256, LANES), 1)
    from_lane = (source >> 4) * 4 + (source & 3)
    lower = jnp.where(from_lane == lane, 1.0, 0.0)
    upper = jnp.where(from_lane + 64 == lane, 1.0, 0.0)

    def merge(rows, hits):
        return jnp.dot(rows, hits, precision=lax.Precision.HIGHEST, preferred_element_type=F32)

    low = merge(kept[0:32], lower).reshape(2, NC, BLK, LANES)
    high = merge(kept[32:64], upper).reshape(2, NC, BLK, LANES)
    for c in range(NC):
        sent = (low[:, c] + high[:, c]).reshape(16, LANES)
        for x in range(NX):
            for head in range(NH):
                out_ref[x, c, head] = sent


def norm_kernel(sums_ref, wide_ref, key_ref, value_ref, out_ref):
    count = 32
    left = iota((count, LANES), 1) < 64
    source, lane = iota((LANES, LANES), 0), iota((LANES, LANES), 1)
    hits = [(lane == (source >> 2) * 8 + c * 4 + (source & 3)) & (source < 64) for c in range(NC)]
    backs = [(source == (lane >> 2) * 8 + c * 4 + (lane & 3)) & (lane < 64) for c in range(NC)]
    shares, gains, biases = [], [], []
    for x in range(NX):
        whole = (
            wide_ref[x, TOK : TOK + 16, :].astype(F32)
            + wide_ref[x, TOK + 16 : TOK + 32, :].astype(F32)
        ) + wide_ref[x, TOK + 32 : WIDE, :].astype(F32)
        for c in range(NC):
            total = sums_ref[x, c, 0]
            for head in range(1, NH):
                total = total + sums_ref[x, c, head]
            total = jnp.concatenate([total, pltpu.roll(total, 64, 1)], 0)
            extra = jnp.dot(
                whole,
                jnp.where(backs[c], 1.0, 0.0),
                precision=lax.Precision.HIGHEST,
                preferred_element_type=F32,
            )
            gains.append(extra[0:1, :])
            biases.append(extra[1:2, :])
            shares.append(jnp.where(left, total + extra[2:3, :], 0.0))
    first = shares[0]
    second = shares[0] * shares[0]
    for share in shares[1:]:
        first = first + share
        second = second + share * share
    center = jnp.sum(first, 1, keepdims=True) * (1.0 / 512)
    spread = jnp.sum(second, 1, keepdims=True) * (1.0 / 512)
    scale = lax.rsqrt(spread - center * center + 1e-05)
    keys = jnp.zeros((count, LANES), F32)
    values = jnp.zeros((count, LANES), F32)
    for x in range(NX):
        natural = None
        for c in range(NC):
            index = x * NC + c
            normed = (shares[index] - center) * scale * gains[index] + biases[index]
            normed = jnp.where(left, normed, 0.0).astype(BF16)
            part = jnp.dot(
                normed, jnp.where(hits[c], 1.0, 0.0).astype(BF16), preferred_element_type=F32
            )
            natural = part if natural is None else natural + part
        natural = natural.astype(BF16)
        keys = keys + jnp.dot(
            natural, key_ref[x * 128 : x * 128 + 128, :], preferred_element_type=F32
        )
        values = values + jnp.dot(
            natural, value_ref[x * 128 : x * 128 + 128, :], preferred_element_type=F32
        )
    both = jnp.concatenate([keys, values], 1).astype(BF16)
    for z in range(NZ):
        out_ref[z] = both


def query_kernel(features_ref, weight_ref, out_ref):
    total = None
    for head in range(NH):
        part = jnp.dot(
            features_ref[head, 0:TOK, :],
            weight_ref[head * 128 : head * 128 + 128, :],
            preferred_element_type=F32,
        )
        total = part if total is None else total + part
    out_ref[...] = total.astype(BF16)


def attend_kernel(query_ref, key_value_ref, weight_ref, mask_ref, out_ref):
    factor = math.log2(math.e) / math.sqrt(64)
    keys = key_value_ref[:, 0:128]
    values = key_value_ref[:, 128:256]
    query = query_ref[...]
    lane, row = iota((TOK, LANES), 1), iota((LANES, TOK), 0)
    mixed = []
    for head in range(2):
        masked = jnp.where((lane >> 6) == head, query.astype(F32), 0.0).astype(BF16)
        scores = lax.dot_general(keys, masked, NT, preferred_element_type=F32)
        highest = jnp.max(scores, 0, keepdims=True)
        weights = jnp.exp2((scores - highest) * factor)
        totals = jnp.sum(weights, 0, keepdims=True)
        mix = lax.dot_general(values, weights.astype(BF16), TN, preferred_element_type=F32)
        mixed.append(mix / totals)
    attended = jnp.where(row < 64, mixed[0], mixed[1])
    attended = jnp.where(mask_ref[...] != 0, attended, 0.0).astype(BF16)
    part = lax.dot_general(attended, weight_ref[...], TN, preferred_element_type=F32).astype(BF16)
    for group in range(NH):
        out_ref[group] = part[:, group * 128 : group * 128 + 128]


def local(
    tile_rows,
    tile_order,
    tissue_mask,
    conv_weight,
    conv_bias,
    norm_gain,
    norm_bias,
    query_weight,
    key_weight,
    value_weight,
    out_weight,
):
    shape = jax.ShapeDtypeStruct
    hbm = pl.BlockSpec(memory_space=pl.ANY)
    sorted_rows, wide, most = pl.pallas_call(
        route_kernel,
        out_shape=(
            shape((NZ, SEND, LANES), BF16),
            shape((WIDE, LANES), BF16),
            shape((MOST, LANES), BF16),
        ),
        in_specs=[hbm] * 7,
        scratch_shapes=[
            pltpu.VMEM((TOK, LANES), BF16),
            pltpu.VMEM((1, TOK), jnp.int32),
            pltpu.VMEM((1, TOK), jnp.int32),
            pltpu.VMEM((256, LANES), BF16),
            pltpu.VMEM((1, LANES), F32),
            pltpu.VMEM((1, LANES), F32),
            pltpu.VMEM((1, LANES), F32),
            pltpu.SemaphoreType.DMA((7,)),
        ],
        compiler_params=params(60),
    )(
        tile_rows,
        tile_order.reshape(1, TOK),
        tissue_mask.reshape(1, TOK),
        conv_weight.reshape(256, LANES),
        norm_gain.reshape(1, LANES),
        norm_bias.reshape(1, LANES),
        conv_bias.reshape(1, LANES),
    )
    arrived = lax.all_to_all(sorted_rows, "z", split_axis=0, concat_axis=0, tiled=True)
    features = lax.all_gather(wide, "head", axis=0)
    queries = pl.pallas_call(
        query_kernel, out_shape=shape((TOK, LANES), BF16), compiler_params=params(16)
    )(features, query_weight)
    arrived, most, queries = lax.optimization_barrier((arrived, most, queries))
    weights = lax.all_gather(most, "z", axis=0, tiled=True).reshape(NZ, MOST, LANES)
    both = lax.all_gather(arrived, "core", axis=0)
    payload = both[:, :, :ROWS].reshape(NC, NZ, PLANE, SLOTS, LANES).transpose(0, 2, 1, 3, 4)
    places = both[:, :, ROWS, :ROWS].reshape(NC, NZ, PLANE, SLOTS).transpose(0, 2, 1, 3)
    places = jnp.pad(places.reshape(NC, PLANE, LANES), ((0, 0), (0, 8), (0, 0)))
    here = jnp.concatenate([payload.reshape(NC, PLANE * 128, LANES), places], 1)
    tiles = lax.all_to_all(
        jnp.broadcast_to(here[None], (NX,) + here.shape), "x", split_axis=0, concat_axis=0, tiled=True
    )
    tail = arrived[:, ROWS + 8 :]
    patches = pl.pallas_call(
        place_kernel,
        out_shape=shape((PATCH, 64, LANES), BF16),
        scratch_shapes=[pltpu.VMEM((PATCH, 64, LANES), F32)],
        compiler_params=params(24),
    )(tiles)
    partial = pl.pallas_call(
        conv_kernel,
        out_shape=shape((NX, NC, NH, 16, LANES), F32),
        compiler_params=params(16),
    )(patches, weights, tail)
    sums = lax.all_to_all(
        partial.reshape(PLANE * NH, 16, LANES),
        ("x", "core", "head"),
        split_axis=0,
        concat_axis=0,
        tiled=True,
    )
    key_value = pl.pallas_call(
        norm_kernel, out_shape=shape((NZ, 32, 256), BF16), compiler_params=params(16)
    )(sums.reshape(NX, NC, NH, 16, LANES), features, key_weight, value_weight)
    gathered = lax.all_to_all(key_value, "z", split_axis=0, concat_axis=0, tiled=True)
    gathered = lax.all_gather(gathered.reshape(NZ * 32, 256), "core", axis=0, tiled=True)
    parts = pl.pallas_call(
        attend_kernel, out_shape=shape((NH, TOK, LANES), BF16), compiler_params=params(24)
    )(queries, gathered, out_weight, tissue_mask.reshape(1, TOK))
    parts = lax.all_to_all(parts, "head", split_axis=0, concat_axis=0, tiled=True)
    return jnp.sum(parts.astype(F32), 0).astype(BF16)


def solution(mesh):
    grid = Mesh(mesh.devices.reshape(NX, NZ, NC, NH), ("x", "z", "core", "head"))
    seq = ("x", "z", "core")
    return jax.shard_map(
        local,
        mesh=grid,
        in_specs=(
            P(seq, "head"),
            P(seq),
            P(seq),
            P(seq, None, "head"),
            P("head"),
            P("head"),
            P("head"),
            P(None, "head"),
            P(None, "head"),
            P(None, "head"),
            P("head", None),
        ),
        out_specs=P(seq, "head"),
        check_vma=False,
    )
```

```python
import math

import jax
import jax.numpy as jnp
from jax import lax
from jax.experimental import pallas as pl
from jax.experimental.pallas import tpu as pltpu
from jax.sharding import Mesh
from jax.sharding import PartitionSpec as P

NX, NZ, NC, NH = 4, 16, 2, 4
PLANE = NX * NC
SLOTS = 8
ROWS = PLANE * SLOTS
SEND = ROWS + 16
TOK = 512
MOST = 248
WIDE = TOK + 48
LANES = 128
BLK = 8
PATCH = 64
EMPTY = 1024.0
HERE = PLANE * 128 + 16
F32 = jnp.float32
BF16 = jnp.bfloat16
NT = (((1,), (1,)), ((), ()))
TN = (((0,), (0,)), ((), ()))


def params(mib):
    return pltpu.CompilerParams(vmem_limit_bytes=mib * 1024 * 1024)


def iota(shape, dim):
    return lax.broadcasted_iota(jnp.int32, shape, dim)


def route_kernel(
    rows_hbm, order_hbm, mask_hbm, kernel_hbm, gain_hbm, shift_hbm, bias_hbm,
    out_ref, wide_ref, most_ref,
    rows_ref, order_ref, mask_ref, kernel_ref, gain_ref, shift_ref, bias_ref, sems,
):
    pairs = (
        (order_hbm, order_ref),
        (mask_hbm, mask_ref),
        (rows_hbm, rows_ref),
        (kernel_hbm, kernel_ref),
        (gain_hbm, gain_ref),
        (shift_hbm, shift_ref),
        (bias_hbm, bias_ref),
    )
    copies = [
        pltpu.make_async_copy(source, held, sems.at[index])
        for index, (source, held) in enumerate(pairs)
    ]
    for copy in copies:
        copy.start()
    before = jnp.where(iota((TOK, TOK), 0) < iota((TOK, TOK), 1), 1.0, 0.0).astype(BF16)
    row256, lane256 = iota((256, 256), 0), iota((256, 256), 1)
    turn = jnp.where(lane256 == (row256 & 3) * PATCH + (row256 >> 2), 1.0, 0.0).astype(BF16)
    for copy in copies:
        copy.wait()
    wide_ref[0:TOK, :] = rows_ref[...]
    whole = jnp.concatenate(
        [gain_ref[...], shift_ref[...], bias_ref[...], jnp.zeros((13, LANES), F32)], 0
    )
    high = whole.astype(BF16)
    rest = whole - high.astype(F32)
    middle = rest.astype(BF16)
    low = (rest - middle.astype(F32)).astype(BF16)
    wide_ref[TOK : TOK + 16, :] = high
    wide_ref[TOK + 16 : TOK + 32, :] = middle
    wide_ref[TOK + 32 : WIDE, :] = low
    turned = jnp.dot(turn, kernel_ref[...], preferred_element_type=F32)
    most_ref[...] = turned[0:MOST, :].astype(BF16)
    tail = turned[MOST:256, :]
    order = order_ref[...]
    row, col = order >> 9, order & 511
    owner = (row >> 3) * 8 + (col >> 6)
    plane = (owner >> 1) & 15
    place = (owner >> 5) * 2 + (owner & 1)
    target = ((row & 7) * 8 + (col & 7)) * BLK + ((col >> 3) & 7)
    code = plane * PLANE + place
    onehot = jnp.where(iota((128, TOK), 0) == code, 1.0, 0.0)
    counts = jnp.dot(onehot.astype(BF16), before, preferred_element_type=F32)
    rank = jnp.sum(onehot * counts, 0, keepdims=True).astype(jnp.int32)
    slot = place * SLOTS + rank
    mine = lax.axis_index("z")
    lane_of = jnp.where(iota((LANES, TOK), 0) == mine * SLOTS + rank, 1.0, 0.0).astype(BF16)
    value = (onehot * (target - 256).astype(F32)).astype(BF16)
    values = lax.dot_general(value, lane_of, NT, preferred_element_type=F32)
    valid = lax.dot_general(onehot.astype(BF16), lane_of, NT, preferred_element_type=F32)
    empty = jnp.where((iota((128, LANES), 1) >> 3) == mine, EMPTY, 0.0)
    meta = jnp.where(valid > 0.5, values, empty)
    wanted = jnp.where(mask_ref[...] != 0, plane * ROWS + slot, -1)
    rows = rows_ref[...]
    for z in range(NZ):
        pick = jnp.where(iota((ROWS, TOK), 0) + z * ROWS == wanted, 1.0, 0.0).astype(BF16)
        out_ref[z, 0:ROWS, :] = jnp.dot(pick, rows, preferred_element_type=F32).astype(BF16)
        last = jnp.concatenate([meta[z * PLANE : z * PLANE + PLANE, :], tail], 0)
        out_ref[z, ROWS:SEND, :] = last.astype(BF16)


def spread_kernel(arrived_ref, out_hbm, here_ref, sems):
    for owner in range(PLANE):
        rows = arrived_ref[:, owner * SLOTS : owner * SLOTS + SLOTS, :]
        here_ref[owner * 128 : owner * 128 + 128, :] = rows.reshape(128, LANES)
    places = arrived_ref[0, ROWS:SEND, :].astype(F32)
    for z in range(1, NZ):
        places = places + arrived_ref[z, ROWS:SEND, :].astype(F32)
    here_ref[PLANE * 128 : HERE, :] = places.astype(BF16)
    copies = [
        pltpu.make_async_copy(here_ref, out_hbm.at[index], sems.at[index])
        for index in range(PLANE)
    ]
    for copy in copies:
        copy.start()
    for copy in copies:
        copy.wait()


def place_kernel(tile_ref, out_ref, patch_ref):
    spot = (iota((TOK, LANES), 0) - 256).astype(F32)
    metas = [
        tile_ref[source, PLANE * 128 : HERE, :].astype(F32) for source in range(PLANE)
    ]
    for owner in range(PLANE):
        picks, tiles = [], []
        for source in range(PLANE):
            meta = metas[source][owner : owner + 1, :]
            picks.append(jnp.where(spot == meta, 1.0, 0.0).astype(BF16))
            tiles.append(tile_ref[source, owner * 128 : owner * 128 + 128, :])
        total = jnp.dot(
            jnp.concatenate(picks, 1), jnp.concatenate(tiles, 0), preferred_element_type=F32
        )
        patch_ref[:, owner * BLK : owner * BLK + BLK, :] = total.reshape(PATCH, BLK, LANES)
    out_ref[...] = patch_ref[...].astype(BF16)


def conv_kernel(patch_ref, weight_ref, tail_ref, out_ref):
    acc = jnp.zeros((256, 256), F32)
    for quad in range(16):
        if quad < 15:
            left = weight_ref[:, quad * 16 : quad * 16 + 16, :]
        else:
            most = weight_ref[:, quad * 16 : MOST, :].astype(F32)
            left = jnp.concatenate([most, tail_ref[...].astype(F32)], 1).astype(BF16)
        left = left.reshape(256, LANES)
        right = patch_ref[quad * 4 : quad * 4 + 4, :, :].reshape(256, LANES)
        acc = acc + lax.dot_general(right, left, NT, preferred_element_type=F32)
    column = iota((64, 256), 1)
    kept = jnp.zeros((64, 256), F32)
    for step in range(4):
        kept = kept + jnp.where(
            ((column >> 2) & 3) == step, acc[step * 64 : step * 64 + 64, :], 0.0
        )
    source, lane = iota((256, LANES), 0), iota((256, LANES), 1)
    from_lane = (source >> 4) * 4 + (source & 3)
    lower = jnp.where(from_lane == lane, 1.0, 0.0)
    upper = jnp.where(from_lane + 64 == lane, 1.0, 0.0)

    def merge(rows, hits):
        return jnp.dot(rows, hits, precision=lax.Precision.HIGHEST, preferred_element_type=F32)

    low = merge(kept[0:32], lower).reshape(2, NC, BLK, LANES)
    high = merge(kept[32:64], upper).reshape(2, NC, BLK, LANES)
    for c in range(NC):
        sent = (low[:, c] + high[:, c]).reshape(16, LANES)
        for x in range(NX):
            for head in range(NH):
                out_ref[x, c, head] = sent


def norm_kernel(sums_ref, wide_ref, key_ref, value_ref, out_ref):
    count = 32
    left = iota((count, LANES), 1) < 64
    source, lane = iota((LANES, LANES), 0), iota((LANES, LANES), 1)
    hits = [(lane == (source >> 2) * 8 + c * 4 + (source & 3)) & (source < 64) for c in range(NC)]
    backs = [(source == (lane >> 2) * 8 + c * 4 + (lane & 3)) & (lane < 64) for c in range(NC)]
    shares, gains, biases = [], [], []
    for x in range(NX):
        whole = (
            wide_ref[x, TOK : TOK + 16, :].astype(F32)
            + wide_ref[x, TOK + 16 : TOK + 32, :].astype(F32)
        ) + wide_ref[x, TOK + 32 : WIDE, :].astype(F32)
        for c in range(NC):
            total = sums_ref[x, c, 0]
            for head in range(1, NH):
                total = total + sums_ref[x, c, head]
            total = jnp.concatenate([total, pltpu.roll(total, 64, 1)], 0)
            extra = jnp.dot(
                whole,
                jnp.where(backs[c], 1.0, 0.0),
                precision=lax.Precision.HIGHEST,
                preferred_element_type=F32,
            )
            gains.append(extra[0:1, :])
            biases.append(extra[1:2, :])
            shares.append(jnp.where(left, total + extra[2:3, :], 0.0))
    first = shares[0]
    second = shares[0] * shares[0]
    for share in shares[1:]:
        first = first + share
        second = second + share * share
    center = jnp.sum(first, 1, keepdims=True) * (1.0 / 512)
    spread = jnp.sum(second, 1, keepdims=True) * (1.0 / 512)
    scale = lax.rsqrt(spread - center * center + 1e-05)
    keys = jnp.zeros((count, LANES), F32)
    values = jnp.zeros((count, LANES), F32)
    for x in range(NX):
        natural = None
        for c in range(NC):
            index = x * NC + c
            normed = (shares[index] - center) * scale * gains[index] + biases[index]
            normed = jnp.where(left, normed, 0.0).astype(BF16)
            part = jnp.dot(
                normed, jnp.where(hits[c], 1.0, 0.0).astype(BF16), preferred_element_type=F32
            )
            natural = part if natural is None else natural + part
        natural = natural.astype(BF16)
        keys = keys + jnp.dot(
            natural, key_ref[x * 128 : x * 128 + 128, :], preferred_element_type=F32
        )
        values = values + jnp.dot(
            natural, value_ref[x * 128 : x * 128 + 128, :], preferred_element_type=F32
        )
    both = jnp.concatenate([keys, values], 1).astype(BF16)
    for z in range(NZ):
        out_ref[z] = both


def query_kernel(features_ref, weight_ref, out_ref):
    total = None
    for head in range(NH):
        part = jnp.dot(
            features_ref[head, 0:TOK, :],
            weight_ref[head * 128 : head * 128 + 128, :],
            preferred_element_type=F32,
        )
        total = part if total is None else total + part
    out_ref[...] = total.astype(BF16)


def attend_kernel(query_ref, key_value_ref, weight_ref, mask_ref, out_ref):
    factor = math.log2(math.e) / math.sqrt(64)
    keys = key_value_ref[:, 0:128]
    values = key_value_ref[:, 128:256]
    query = query_ref[...]
    lane, row = iota((TOK, LANES), 1), iota((LANES, TOK), 0)
    mixed = []
    for head in range(2):
        masked = jnp.where((lane >> 6) == head, query.astype(F32), 0.0).astype(BF16)
        scores = lax.dot_general(keys, masked, NT, preferred_element_type=F32)
        highest = jnp.max(scores, 0, keepdims=True)
        weights = jnp.exp2((scores - highest) * factor)
        totals = jnp.sum(weights, 0, keepdims=True)
        mix = lax.dot_general(values, weights.astype(BF16), TN, preferred_element_type=F32)
        mixed.append(mix / totals)
    attended = jnp.where(row < 64, mixed[0], mixed[1])
    attended = jnp.where(mask_ref[...] != 0, attended, 0.0).astype(BF16)
    part = lax.dot_general(attended, weight_ref[...], TN, preferred_element_type=F32).astype(BF16)
    for group in range(NH):
        out_ref[group] = part[:, group * 128 : group * 128 + 128]


def local(
    tile_rows,
    tile_order,
    tissue_mask,
    conv_weight,
    conv_bias,
    norm_gain,
    norm_bias,
    query_weight,
    key_weight,
    value_weight,
    out_weight,
):
    shape = jax.ShapeDtypeStruct
    hbm = pl.BlockSpec(memory_space=pl.ANY)
    sorted_rows, wide, most = pl.pallas_call(
        route_kernel,
        out_shape=(
            shape((NZ, SEND, LANES), BF16),
            shape((WIDE, LANES), BF16),
            shape((MOST, LANES), BF16),
        ),
        in_specs=[hbm] * 7,
        scratch_shapes=[
            pltpu.VMEM((TOK, LANES), BF16),
            pltpu.VMEM((1, TOK), jnp.int32),
            pltpu.VMEM((1, TOK), jnp.int32),
            pltpu.VMEM((256, LANES), BF16),
            pltpu.VMEM((1, LANES), F32),
            pltpu.VMEM((1, LANES), F32),
            pltpu.VMEM((1, LANES), F32),
            pltpu.SemaphoreType.DMA((7,)),
        ],
        compiler_params=params(60),
    )(
        tile_rows,
        tile_order.reshape(1, TOK),
        tissue_mask.reshape(1, TOK),
        conv_weight.reshape(256, LANES),
        norm_gain.reshape(1, LANES),
        norm_bias.reshape(1, LANES),
        conv_bias.reshape(1, LANES),
    )
    arrived = lax.all_to_all(sorted_rows, "z", split_axis=0, concat_axis=0, tiled=True)
    features = lax.all_gather(wide, "head", axis=0)
    queries = pl.pallas_call(
        query_kernel, out_shape=shape((TOK, LANES), BF16), compiler_params=params(16)
    )(features, query_weight)
    arrived, most, queries = lax.optimization_barrier((arrived, most, queries))
    weights = lax.all_gather(most, "z", axis=0, tiled=True).reshape(NZ, MOST, LANES)
    spread = pl.pallas_call(
        spread_kernel,
        out_shape=shape((PLANE, HERE, LANES), BF16),
        out_specs=hbm,
        scratch_shapes=[pltpu.VMEM((HERE, LANES), BF16), pltpu.SemaphoreType.DMA((PLANE,))],
        compiler_params=params(16),
    )(arrived)
    tiles = lax.all_to_all(spread, ("x", "core"), split_axis=0, concat_axis=0, tiled=True)
    tail = arrived[:, ROWS + 8 :]
    patches = pl.pallas_call(
        place_kernel,
        out_shape=shape((PATCH, 64, LANES), BF16),
        scratch_shapes=[pltpu.VMEM((PATCH, 64, LANES), F32)],
        compiler_params=params(24),
    )(tiles)
    partial = pl.pallas_call(
        conv_kernel,
        out_shape=shape((NX, NC, NH, 16, LANES), F32),
        compiler_params=params(16),
    )(patches, weights, tail)
    sums = lax.all_to_all(
        partial.reshape(PLANE * NH, 16, LANES),
        ("x", "core", "head"),
        split_axis=0,
        concat_axis=0,
        tiled=True,
    )
    key_value = pl.pallas_call(
        norm_kernel, out_shape=shape((NZ, 32, 256), BF16), compiler_params=params(16)
    )(sums.reshape(NX, NC, NH, 16, LANES), features, key_weight, value_weight)
    gathered = lax.all_to_all(key_value, "z", split_axis=0, concat_axis=0, tiled=True)
    gathered = lax.all_gather(gathered.reshape(NZ * 32, 256), "core", axis=0, tiled=True)
    parts = pl.pallas_call(
        attend_kernel, out_shape=shape((NH, TOK, LANES), BF16), compiler_params=params(24)
    )(queries, gathered, out_weight, tissue_mask.reshape(1, TOK))
    parts = lax.all_to_all(parts, "head", split_axis=0, concat_axis=0, tiled=True)
    return jnp.sum(parts.astype(F32), 0).astype(BF16)


def solution(mesh):
    grid = Mesh(mesh.devices.reshape(NX, NZ, NC, NH), ("x", "z", "core", "head"))
    seq = ("x", "z", "core")
    return jax.shard_map(
        local,
        mesh=grid,
        in_specs=(
            P(seq, "head"),
            P(seq),
            P(seq),
            P(seq, None, "head"),
            P("head"),
            P("head"),
            P("head"),
            P(None, "head"),
            P(None, "head"),
            P(None, "head"),
            P("head", None),
        ),
        out_specs=P(seq, "head"),
        check_vma=False,
    )
```

```python
import math

import jax
import jax.numpy as jnp
from jax import lax
from jax.experimental import pallas as pl
from jax.experimental.pallas import tpu as pltpu
from jax.sharding import Mesh
from jax.sharding import PartitionSpec as P

NX, NZ, NC, NH = 4, 16, 2, 4
PLANE = NX * NC
SLOTS = 8
ROWS = PLANE * SLOTS
SEND = ROWS + 8
TOK = 512
MOST = 252
WIDE = TOK + 48
LANES = 128
BLK = 8
PATCH = 64
EMPTY = 1024.0
HERE = PLANE * 128 + 16
F32 = jnp.float32
BF16 = jnp.bfloat16
NT = (((1,), (1,)), ((), ()))
TN = (((0,), (0,)), ((), ()))


def params(mib):
    return pltpu.CompilerParams(vmem_limit_bytes=mib * 1024 * 1024)


def iota(shape, dim):
    return lax.broadcasted_iota(jnp.int32, shape, dim)


def route_kernel(
    rows_hbm, order_hbm, mask_hbm, kernel_hbm, gain_hbm, shift_hbm, bias_hbm,
    out_ref, wide_ref, most_ref,
    rows_ref, order_ref, mask_ref, kernel_ref, gain_ref, shift_ref, bias_ref, sems,
):
    pairs = (
        (order_hbm, order_ref),
        (mask_hbm, mask_ref),
        (rows_hbm, rows_ref),
        (kernel_hbm, kernel_ref),
        (gain_hbm, gain_ref),
        (shift_hbm, shift_ref),
        (bias_hbm, bias_ref),
    )
    copies = [
        pltpu.make_async_copy(source, held, sems.at[index])
        for index, (source, held) in enumerate(pairs)
    ]
    for copy in copies:
        copy.start()
    before = jnp.where(iota((TOK, TOK), 0) < iota((TOK, TOK), 1), 1.0, 0.0).astype(BF16)
    row256, lane256 = iota((256, 256), 0), iota((256, 256), 1)
    turn = jnp.where(lane256 == (row256 & 3) * PATCH + (row256 >> 2), 1.0, 0.0).astype(BF16)
    for copy in copies:
        copy.wait()
    wide_ref[0:TOK, :] = rows_ref[...]
    whole = jnp.concatenate(
        [gain_ref[...], shift_ref[...], bias_ref[...], jnp.zeros((13, LANES), F32)], 0
    )
    high = whole.astype(BF16)
    rest = whole - high.astype(F32)
    middle = rest.astype(BF16)
    low = (rest - middle.astype(F32)).astype(BF16)
    wide_ref[TOK : TOK + 16, :] = high
    wide_ref[TOK + 16 : TOK + 32, :] = middle
    wide_ref[TOK + 32 : WIDE, :] = low
    turned = jnp.dot(turn, kernel_ref[...], preferred_element_type=F32)
    most_ref[...] = turned[0:MOST, :].astype(BF16)
    tail = turned[MOST - 4 : 256, :]
    lower = iota((8, LANES), 0) < 4
    order = order_ref[...]
    row, col = order >> 9, order & 511
    owner = (row >> 3) * 8 + (col >> 6)
    plane = (owner >> 1) & 15
    place = (owner >> 5) * 2 + (owner & 1)
    target = ((row & 7) * 8 + (col & 7)) * BLK + ((col >> 3) & 7)
    code = plane * PLANE + place
    onehot = jnp.where(iota((128, TOK), 0) == code, 1.0, 0.0)
    counts = jnp.dot(onehot.astype(BF16), before, preferred_element_type=F32)
    rank = jnp.sum(onehot * counts, 0, keepdims=True).astype(jnp.int32)
    slot = place * SLOTS + rank
    here = iota((NZ, TOK), 0) == plane
    value = jnp.where(here, (target - 256).astype(F32), 0.0).astype(BF16)
    there = jnp.where(here, 1.0, 0.0).astype(BF16)
    lane_of = jnp.where(iota((LANES, TOK), 0) == slot, 1.0, 0.0).astype(BF16)
    values = lax.dot_general(value, lane_of, NT, preferred_element_type=F32)
    valid = lax.dot_general(there, lane_of, NT, preferred_element_type=F32)
    meta = jnp.where(valid > 0.5, values, EMPTY)
    wanted = jnp.where(mask_ref[...] != 0, plane * ROWS + slot, -1)
    rows = rows_ref[...]
    for z in range(NZ):
        pick = jnp.where(iota((ROWS, TOK), 0) + z * ROWS == wanted, 1.0, 0.0).astype(BF16)
        out_ref[z, 0:ROWS, :] = jnp.dot(pick, rows, preferred_element_type=F32).astype(BF16)
        last = jnp.where(lower, jnp.broadcast_to(meta[z : z + 1, :], (8, LANES)), tail)
        out_ref[z, ROWS:SEND, :] = last.astype(BF16)


def spread_kernel(arrived_ref, out_hbm, here_ref, sems):
    for owner in range(PLANE):
        rows = arrived_ref[:, owner * SLOTS : owner * SLOTS + SLOTS, :]
        here_ref[owner * 128 : owner * 128 + 128, :] = rows.reshape(128, LANES)
    last = arrived_ref[:, ROWS:SEND, :].astype(F32)
    rows = jnp.concatenate([last[z, 0:1, :] for z in range(NZ)], 0).astype(BF16)
    source, lane = iota((LANES, LANES), 0), iota((LANES, LANES), 1)
    own = iota((NZ, LANES), 0) == (iota((NZ, LANES), 1) >> 3)
    found = []
    for owner in range(PLANE):
        pick = jnp.where(source == owner * SLOTS + (lane & 7), 1.0, 0.0).astype(BF16)
        moved = jnp.dot(rows, pick, preferred_element_type=F32)
        found.append(jnp.sum(jnp.where(own, moved, 0.0), 0, keepdims=True))
    found.append(jnp.zeros((8, LANES), F32))
    here_ref[PLANE * 128 : HERE, :] = jnp.concatenate(found, 0).astype(BF16)
    copies = [
        pltpu.make_async_copy(here_ref, out_hbm.at[index], sems.at[index])
        for index in range(PLANE)
    ]
    for copy in copies:
        copy.start()
    for copy in copies:
        copy.wait()


def place_kernel(tile_ref, out_ref, patch_ref):
    spot = (iota((TOK, LANES), 0) - 256).astype(F32)
    metas = [
        tile_ref[source, PLANE * 128 : HERE, :].astype(F32) for source in range(PLANE)
    ]
    for owner in range(PLANE):
        picks, tiles = [], []
        for source in range(PLANE):
            meta = metas[source][owner : owner + 1, :]
            picks.append(jnp.where(spot == meta, 1.0, 0.0).astype(BF16))
            tiles.append(tile_ref[source, owner * 128 : owner * 128 + 128, :])
        total = jnp.dot(
            jnp.concatenate(picks, 1), jnp.concatenate(tiles, 0), preferred_element_type=F32
        )
        patch_ref[:, owner * BLK : owner * BLK + BLK, :] = total.reshape(PATCH, BLK, LANES)
    out_ref[...] = patch_ref[...].astype(BF16)


def conv_kernel(patch_ref, weight_ref, tail_ref, out_ref):
    acc = jnp.zeros((256, 256), F32)
    for quad in range(16):
        if quad < 15:
            left = weight_ref[:, quad * 16 : quad * 16 + 16, :]
        else:
            most = weight_ref[:, quad * 16 : MOST, :].astype(F32)
            left = jnp.concatenate([most, tail_ref[:, 4:8, :].astype(F32)], 1).astype(BF16)
        left = left.reshape(256, LANES)
        right = patch_ref[quad * 4 : quad * 4 + 4, :, :].reshape(256, LANES)
        acc = acc + lax.dot_general(right, left, NT, preferred_element_type=F32)
    column = iota((64, 256), 1)
    kept = jnp.zeros((64, 256), F32)
    for step in range(4):
        kept = kept + jnp.where(
            ((column >> 2) & 3) == step, acc[step * 64 : step * 64 + 64, :], 0.0
        )
    source, lane = iota((256, LANES), 0), iota((256, LANES), 1)
    from_lane = (source >> 4) * 4 + (source & 3)
    lower = jnp.where(from_lane == lane, 1.0, 0.0)
    upper = jnp.where(from_lane + 64 == lane, 1.0, 0.0)

    def merge(rows, hits):
        return jnp.dot(rows, hits, precision=lax.Precision.HIGHEST, preferred_element_type=F32)

    low = merge(kept[0:32], lower).reshape(2, NC, BLK, LANES)
    high = merge(kept[32:64], upper).reshape(2, NC, BLK, LANES)
    for c in range(NC):
        sent = (low[:, c] + high[:, c]).reshape(16, LANES)
        for x in range(NX):
            for head in range(NH):
                out_ref[x, c, head] = sent


def norm_kernel(sums_ref, wide_ref, key_ref, value_ref, out_ref):
    count = 32
    left = iota((count, LANES), 1) < 64
    source, lane = iota((LANES, LANES), 0), iota((LANES, LANES), 1)
    hits = [(lane == (source >> 2) * 8 + c * 4 + (source & 3)) & (source < 64) for c in range(NC)]
    backs = [(source == (lane >> 2) * 8 + c * 4 + (lane & 3)) & (lane < 64) for c in range(NC)]
    shares, gains, biases = [], [], []
    for x in range(NX):
        whole = (
            wide_ref[x, TOK : TOK + 16, :].astype(F32)
            + wide_ref[x, TOK + 16 : TOK + 32, :].astype(F32)
        ) + wide_ref[x, TOK + 32 : WIDE, :].astype(F32)
        for c in range(NC):
            total = sums_ref[x, c, 0]
            for head in range(1, NH):
                total = total + sums_ref[x, c, head]
            total = jnp.concatenate([total, pltpu.roll(total, 64, 1)], 0)
            extra = jnp.dot(
                whole,
                jnp.where(backs[c], 1.0, 0.0),
                precision=lax.Precision.HIGHEST,
                preferred_element_type=F32,
            )
            gains.append(extra[0:1, :])
            biases.append(extra[1:2, :])
            shares.append(jnp.where(left, total + extra[2:3, :], 0.0))
    first = shares[0]
    second = shares[0] * shares[0]
    for share in shares[1:]:
        first = first + share
        second = second + share * share
    center = jnp.sum(first, 1, keepdims=True) * (1.0 / 512)
    spread = jnp.sum(second, 1, keepdims=True) * (1.0 / 512)
    scale = lax.rsqrt(spread - center * center + 1e-05)
    keys = jnp.zeros((count, LANES), F32)
    values = jnp.zeros((count, LANES), F32)
    for x in range(NX):
        natural = None
        for c in range(NC):
            index = x * NC + c
            normed = (shares[index] - center) * scale * gains[index] + biases[index]
            normed = jnp.where(left, normed, 0.0).astype(BF16)
            part = jnp.dot(
                normed, jnp.where(hits[c], 1.0, 0.0).astype(BF16), preferred_element_type=F32
            )
            natural = part if natural is None else natural + part
        natural = natural.astype(BF16)
        keys = keys + jnp.dot(
            natural, key_ref[x * 128 : x * 128 + 128, :], preferred_element_type=F32
        )
        values = values + jnp.dot(
            natural, value_ref[x * 128 : x * 128 + 128, :], preferred_element_type=F32
        )
    both = jnp.concatenate([keys, values], 1).astype(BF16)
    for z in range(NZ):
        out_ref[z] = both


def query_kernel(features_ref, weight_ref, out_ref):
    total = None
    for head in range(NH):
        part = jnp.dot(
            features_ref[head, 0:TOK, :],
            weight_ref[head * 128 : head * 128 + 128, :],
            preferred_element_type=F32,
        )
        total = part if total is None else total + part
    out_ref[...] = total.astype(BF16)


def attend_kernel(query_ref, key_value_ref, weight_ref, mask_ref, out_ref):
    factor = math.log2(math.e) / math.sqrt(64)
    keys = key_value_ref[:, 0:128]
    values = key_value_ref[:, 128:256]
    query = query_ref[...]
    lane, row = iota((TOK, LANES), 1), iota((LANES, TOK), 0)
    mixed = []
    for head in range(2):
        masked = jnp.where((lane >> 6) == head, query.astype(F32), 0.0).astype(BF16)
        scores = lax.dot_general(keys, masked, NT, preferred_element_type=F32)
        highest = jnp.max(scores, 0, keepdims=True)
        weights = jnp.exp2((scores - highest) * factor)
        totals = jnp.sum(weights, 0, keepdims=True)
        mix = lax.dot_general(values, weights.astype(BF16), TN, preferred_element_type=F32)
        mixed.append(mix / totals)
    attended = jnp.where(row < 64, mixed[0], mixed[1])
    attended = jnp.where(mask_ref[...] != 0, attended, 0.0).astype(BF16)
    part = lax.dot_general(attended, weight_ref[...], TN, preferred_element_type=F32).astype(BF16)
    for group in range(NH):
        out_ref[group] = part[:, group * 128 : group * 128 + 128]


def local(
    tile_rows,
    tile_order,
    tissue_mask,
    conv_weight,
    conv_bias,
    norm_gain,
    norm_bias,
    query_weight,
    key_weight,
    value_weight,
    out_weight,
):
    shape = jax.ShapeDtypeStruct
    hbm = pl.BlockSpec(memory_space=pl.ANY)
    sorted_rows, wide, most = pl.pallas_call(
        route_kernel,
        out_shape=(
            shape((NZ, SEND, LANES), BF16),
            shape((WIDE, LANES), BF16),
            shape((MOST, LANES), BF16),
        ),
        in_specs=[hbm] * 7,
        scratch_shapes=[
            pltpu.VMEM((TOK, LANES), BF16),
            pltpu.VMEM((1, TOK), jnp.int32),
            pltpu.VMEM((1, TOK), jnp.int32),
            pltpu.VMEM((256, LANES), BF16),
            pltpu.VMEM((1, LANES), F32),
            pltpu.VMEM((1, LANES), F32),
            pltpu.VMEM((1, LANES), F32),
            pltpu.SemaphoreType.DMA((7,)),
        ],
        compiler_params=params(60),
    )(
        tile_rows,
        tile_order.reshape(1, TOK),
        tissue_mask.reshape(1, TOK),
        conv_weight.reshape(256, LANES),
        norm_gain.reshape(1, LANES),
        norm_bias.reshape(1, LANES),
        conv_bias.reshape(1, LANES),
    )
    arrived = lax.all_to_all(sorted_rows, "z", split_axis=0, concat_axis=0, tiled=True)
    features = lax.all_gather(wide, "head", axis=0)
    queries = pl.pallas_call(
        query_kernel, out_shape=shape((TOK, LANES), BF16), compiler_params=params(16)
    )(features, query_weight)
    arrived, most, queries = lax.optimization_barrier((arrived, most, queries))
    weights = lax.all_gather(most, "z", axis=0)
    spread = pl.pallas_call(
        spread_kernel,
        out_shape=shape((PLANE, HERE, LANES), BF16),
        out_specs=hbm,
        scratch_shapes=[pltpu.VMEM((HERE, LANES), BF16), pltpu.SemaphoreType.DMA((PLANE,))],
        compiler_params=params(16),
    )(arrived)
    tiles = lax.all_to_all(spread, ("x", "core"), split_axis=0, concat_axis=0, tiled=True)
    tail = arrived[:, ROWS:]
    patches = pl.pallas_call(
        place_kernel,
        out_shape=shape((PATCH, 64, LANES), BF16),
        scratch_shapes=[pltpu.VMEM((PATCH, 64, LANES), F32)],
        compiler_params=params(24),
    )(tiles)
    partial = pl.pallas_call(
        conv_kernel,
        out_shape=shape((NX, NC, NH, 16, LANES), F32),
        compiler_params=params(16),
    )(patches, weights, tail)
    sums = lax.all_to_all(
        partial.reshape(PLANE * NH, 16, LANES),
        ("x", "core", "head"),
        split_axis=0,
        concat_axis=0,
        tiled=True,
    )
    key_value = pl.pallas_call(
        norm_kernel, out_shape=shape((NZ, 32, 256), BF16), compiler_params=params(16)
    )(sums.reshape(NX, NC, NH, 16, LANES), features, key_weight, value_weight)
    gathered = lax.all_to_all(key_value, "z", split_axis=0, concat_axis=0, tiled=True)
    gathered = lax.all_gather(gathered.reshape(NZ * 32, 256), "core", axis=0, tiled=True)
    parts = pl.pallas_call(
        attend_kernel, out_shape=shape((NH, TOK, LANES), BF16), compiler_params=params(24)
    )(queries, gathered, out_weight, tissue_mask.reshape(1, TOK))
    parts = lax.all_to_all(parts, "head", split_axis=0, concat_axis=0, tiled=True)
    return jnp.sum(parts.astype(F32), 0).astype(BF16)


def solution(mesh):
    grid = Mesh(mesh.devices.reshape(NX, NZ, NC, NH), ("x", "z", "core", "head"))
    seq = ("x", "z", "core")
    return jax.shard_map(
        local,
        mesh=grid,
        in_specs=(
            P(seq, "head"),
            P(seq),
            P(seq),
            P(seq, None, "head"),
            P("head"),
            P("head"),
            P("head"),
            P(None, "head"),
            P(None, "head"),
            P(None, "head"),
            P("head", None),
        ),
        out_specs=P(seq, "head"),
        check_vma=False,
    )
```

```python
import math

import jax
import jax.numpy as jnp
from jax import lax
from jax.experimental import pallas as pl
from jax.experimental.pallas import tpu as pltpu
from jax.sharding import Mesh
from jax.sharding import PartitionSpec as P

NX, NZ, NC, NH = 4, 16, 2, 4
PLANE = NX * NC
SLOTS = 8
ROWS = PLANE * SLOTS
SEND = ROWS + 8
TOK = 512
MOST = 252
WIDE = TOK + 48
LANES = 128
BLK = 8
PATCH = 64
EMPTY = 1024.0
HERE = PLANE * 128 + 16
F32 = jnp.float32
BF16 = jnp.bfloat16
NT = (((1,), (1,)), ((), ()))
TN = (((0,), (0,)), ((), ()))


def params(mib):
    return pltpu.CompilerParams(vmem_limit_bytes=mib * 1024 * 1024)


def iota(shape, dim):
    return lax.broadcasted_iota(jnp.int32, shape, dim)


def route_kernel(
    rows_hbm, order_hbm, mask_hbm, kernel_hbm, gain_hbm, shift_hbm, bias_hbm,
    out_ref, wide_ref, most_ref,
    rows_ref, order_ref, mask_ref, kernel_ref, gain_ref, shift_ref, bias_ref, sems,
):
    pairs = (
        (order_hbm, order_ref),
        (mask_hbm, mask_ref),
        (rows_hbm, rows_ref),
        (kernel_hbm, kernel_ref),
        (gain_hbm, gain_ref),
        (shift_hbm, shift_ref),
        (bias_hbm, bias_ref),
    )
    copies = [
        pltpu.make_async_copy(source, held, sems.at[index])
        for index, (source, held) in enumerate(pairs)
    ]
    for copy in copies:
        copy.start()
    before = jnp.where(iota((TOK, TOK), 0) < iota((TOK, TOK), 1), 1.0, 0.0).astype(BF16)
    row256, lane256 = iota((256, 256), 0), iota((256, 256), 1)
    turn = jnp.where(lane256 == (row256 & 3) * PATCH + (row256 >> 2), 1.0, 0.0).astype(BF16)
    for copy in copies:
        copy.wait()
    wide_ref[0:TOK, :] = rows_ref[...]
    whole = jnp.concatenate(
        [gain_ref[...], shift_ref[...], bias_ref[...], jnp.zeros((13, LANES), F32)], 0
    )
    high = whole.astype(BF16)
    rest = whole - high.astype(F32)
    middle = rest.astype(BF16)
    low = (rest - middle.astype(F32)).astype(BF16)
    wide_ref[TOK : TOK + 16, :] = high
    wide_ref[TOK + 16 : TOK + 32, :] = middle
    wide_ref[TOK + 32 : WIDE, :] = low
    turned = jnp.dot(turn, kernel_ref[...], preferred_element_type=F32)
    most_ref[...] = turned[0:MOST, :].astype(BF16)
    tail = turned[MOST - 4 : 256, :]
    lower = iota((8, LANES), 0) < 4
    order = order_ref[...]
    row, col = order >> 9, order & 511
    owner = (row >> 3) * 8 + (col >> 6)
    plane = (owner >> 1) & 15
    place = (owner >> 5) * 2 + (owner & 1)
    target = ((row & 7) * 8 + (col & 7)) * BLK + ((col >> 3) & 7)
    code = plane * PLANE + place
    onehot = jnp.where(iota((128, TOK), 0) == code, 1.0, 0.0)
    counts = jnp.dot(onehot.astype(BF16), before, preferred_element_type=F32)
    rank = jnp.sum(onehot * counts, 0, keepdims=True).astype(jnp.int32)
    slot = place * SLOTS + rank
    here = iota((NZ, TOK), 0) == plane
    value = jnp.where(here, (target - 256).astype(F32), 0.0).astype(BF16)
    there = jnp.where(here, 1.0, 0.0).astype(BF16)
    lane_of = jnp.where(iota((LANES, TOK), 0) == slot, 1.0, 0.0).astype(BF16)
    values = lax.dot_general(value, lane_of, NT, preferred_element_type=F32)
    valid = lax.dot_general(there, lane_of, NT, preferred_element_type=F32)
    meta = jnp.where(valid > 0.5, values, EMPTY)
    wanted = jnp.where(mask_ref[...] != 0, plane * ROWS + slot, -1)
    rows = rows_ref[...]
    for z in range(NZ):
        pick = jnp.where(iota((ROWS, TOK), 0) + z * ROWS == wanted, 1.0, 0.0).astype(BF16)
        out_ref[z, 0:ROWS, :] = jnp.dot(pick, rows, preferred_element_type=F32).astype(BF16)
        last = jnp.where(lower, jnp.broadcast_to(meta[z : z + 1, :], (8, LANES)), tail)
        out_ref[z, ROWS:SEND, :] = last.astype(BF16)


def spread_kernel(arrived_ref, out_hbm, here_ref, sems):
    for owner in range(PLANE):
        rows = arrived_ref[:, owner * SLOTS : owner * SLOTS + SLOTS, :]
        here_ref[owner * 128 : owner * 128 + 128, :] = rows.reshape(128, LANES)
    last = arrived_ref[:, ROWS:SEND, :].astype(F32)
    rows = jnp.concatenate([last[z, 0:1, :] for z in range(NZ)], 0).astype(BF16)
    source, lane = iota((LANES, LANES), 0), iota((LANES, LANES), 1)
    own = iota((NZ, LANES), 0) == (iota((NZ, LANES), 1) >> 3)
    found = []
    for owner in range(PLANE):
        pick = jnp.where(source == owner * SLOTS + (lane & 7), 1.0, 0.0).astype(BF16)
        moved = jnp.dot(rows, pick, preferred_element_type=F32)
        found.append(jnp.sum(jnp.where(own, moved, 0.0), 0, keepdims=True))
    found.append(jnp.zeros((8, LANES), F32))
    here_ref[PLANE * 128 : HERE, :] = jnp.concatenate(found, 0).astype(BF16)
    copies = [
        pltpu.make_async_copy(here_ref, out_hbm.at[index], sems.at[index])
        for index in range(PLANE)
    ]
    for copy in copies:
        copy.start()
    for copy in copies:
        copy.wait()


def place_kernel(tile_ref, weight_ref, out_ref, patch_ref):
    spot = (iota((TOK, LANES), 0) - 256).astype(F32)
    metas = [
        tile_ref[source, PLANE * 128 : HERE, :].astype(F32) for source in range(PLANE)
    ]
    for owner in range(PLANE):
        picks, tiles = [], []
        for source in range(PLANE):
            meta = metas[source][owner : owner + 1, :]
            picks.append(jnp.where(spot == meta, 1.0, 0.0).astype(BF16))
            tiles.append(tile_ref[source, owner * 128 : owner * 128 + 128, :])
        total = jnp.dot(
            jnp.concatenate(picks, 1), jnp.concatenate(tiles, 0), preferred_element_type=F32
        )
        patch_ref[:, owner * BLK : owner * BLK + BLK, :] = total.reshape(PATCH, BLK, LANES)
    out_ref[...] = patch_ref[...].astype(BF16)


def conv_kernel(patch_ref, weight_ref, tail_ref, out_ref):
    acc = jnp.zeros((256, 256), F32)
    for quad in range(16):
        if quad < 15:
            left = weight_ref[:, quad * 16 : quad * 16 + 16, :]
        else:
            most = weight_ref[:, quad * 16 : MOST, :].astype(F32)
            left = jnp.concatenate([most, tail_ref[:, 4:8, :].astype(F32)], 1).astype(BF16)
        left = left.reshape(256, LANES)
        right = patch_ref[quad * 4 : quad * 4 + 4, :, :].reshape(256, LANES)
        acc = acc + lax.dot_general(right, left, NT, preferred_element_type=F32)
    column = iota((64, 256), 1)
    kept = jnp.zeros((64, 256), F32)
    for step in range(4):
        kept = kept + jnp.where(
            ((column >> 2) & 3) == step, acc[step * 64 : step * 64 + 64, :], 0.0
        )
    source, lane = iota((256, LANES), 0), iota((256, LANES), 1)
    from_lane = (source >> 4) * 4 + (source & 3)
    lower = jnp.where(from_lane == lane, 1.0, 0.0)
    upper = jnp.where(from_lane + 64 == lane, 1.0, 0.0)

    def merge(rows, hits):
        return jnp.dot(rows, hits, precision=lax.Precision.HIGHEST, preferred_element_type=F32)

    low = merge(kept[0:32], lower).reshape(2, NC, BLK, LANES)
    high = merge(kept[32:64], upper).reshape(2, NC, BLK, LANES)
    for c in range(NC):
        sent = (low[:, c] + high[:, c]).reshape(16, LANES)
        for x in range(NX):
            for head in range(NH):
                out_ref[x, c, head] = sent


def norm_kernel(sums_ref, wide_ref, key_ref, value_ref, out_ref):
    count = 32
    left = iota((count, LANES), 1) < 64
    source, lane = iota((LANES, LANES), 0), iota((LANES, LANES), 1)
    hits = [(lane == (source >> 2) * 8 + c * 4 + (source & 3)) & (source < 64) for c in range(NC)]
    backs = [(source == (lane >> 2) * 8 + c * 4 + (lane & 3)) & (lane < 64) for c in range(NC)]
    shares, gains, biases = [], [], []
    for x in range(NX):
        whole = (
            wide_ref[x, TOK : TOK + 16, :].astype(F32)
            + wide_ref[x, TOK + 16 : TOK + 32, :].astype(F32)
        ) + wide_ref[x, TOK + 32 : WIDE, :].astype(F32)
        for c in range(NC):
            total = sums_ref[x, c, 0]
            for head in range(1, NH):
                total = total + sums_ref[x, c, head]
            total = jnp.concatenate([total, pltpu.roll(total, 64, 1)], 0)
            extra = jnp.dot(
                whole,
                jnp.where(backs[c], 1.0, 0.0),
                precision=lax.Precision.HIGHEST,
                preferred_element_type=F32,
            )
            gains.append(extra[0:1, :])
            biases.append(extra[1:2, :])
            shares.append(jnp.where(left, total + extra[2:3, :], 0.0))
    first = shares[0]
    second = shares[0] * shares[0]
    for share in shares[1:]:
        first = first + share
        second = second + share * share
    center = jnp.sum(first, 1, keepdims=True) * (1.0 / 512)
    spread = jnp.sum(second, 1, keepdims=True) * (1.0 / 512)
    scale = lax.rsqrt(spread - center * center + 1e-05)
    keys = jnp.zeros((count, LANES), F32)
    values = jnp.zeros((count, LANES), F32)
    for x in range(NX):
        natural = None
        for c in range(NC):
            index = x * NC + c
            normed = (shares[index] - center) * scale * gains[index] + biases[index]
            normed = jnp.where(left, normed, 0.0).astype(BF16)
            part = jnp.dot(
                normed, jnp.where(hits[c], 1.0, 0.0).astype(BF16), preferred_element_type=F32
            )
            natural = part if natural is None else natural + part
        natural = natural.astype(BF16)
        keys = keys + jnp.dot(
            natural, key_ref[x * 128 : x * 128 + 128, :], preferred_element_type=F32
        )
        values = values + jnp.dot(
            natural, value_ref[x * 128 : x * 128 + 128, :], preferred_element_type=F32
        )
    both = jnp.concatenate([keys, values], 1).astype(BF16)
    for z in range(NZ):
        out_ref[z] = both


def query_kernel(features_ref, weight_ref, out_ref):
    total = None
    for head in range(NH):
        part = jnp.dot(
            features_ref[head, 0:TOK, :],
            weight_ref[head * 128 : head * 128 + 128, :],
            preferred_element_type=F32,
        )
        total = part if total is None else total + part
    out_ref[...] = total.astype(BF16)


def attend_kernel(query_ref, key_value_ref, weight_ref, mask_ref, out_ref):
    factor = math.log2(math.e) / math.sqrt(64)
    keys = key_value_ref[:, 0:128]
    values = key_value_ref[:, 128:256]
    query = query_ref[...]
    lane, row = iota((TOK, LANES), 1), iota((LANES, TOK), 0)
    mixed = []
    for head in range(2):
        masked = jnp.where((lane >> 6) == head, query.astype(F32), 0.0).astype(BF16)
        scores = lax.dot_general(keys, masked, NT, preferred_element_type=F32)
        highest = jnp.max(scores, 0, keepdims=True)
        weights = jnp.exp2((scores - highest) * factor)
        totals = jnp.sum(weights, 0, keepdims=True)
        mix = lax.dot_general(values, weights.astype(BF16), TN, preferred_element_type=F32)
        mixed.append(mix / totals)
    attended = jnp.where(row < 64, mixed[0], mixed[1])
    attended = jnp.where(mask_ref[...] != 0, attended, 0.0).astype(BF16)
    part = lax.dot_general(attended, weight_ref[...], TN, preferred_element_type=F32).astype(BF16)
    for group in range(NH):
        out_ref[group] = part[:, group * 128 : group * 128 + 128]


def local(
    tile_rows,
    tile_order,
    tissue_mask,
    conv_weight,
    conv_bias,
    norm_gain,
    norm_bias,
    query_weight,
    key_weight,
    value_weight,
    out_weight,
):
    shape = jax.ShapeDtypeStruct
    hbm = pl.BlockSpec(memory_space=pl.ANY)
    sorted_rows, wide, most = pl.pallas_call(
        route_kernel,
        out_shape=(
            shape((NZ, SEND, LANES), BF16),
            shape((WIDE, LANES), BF16),
            shape((MOST, LANES), BF16),
        ),
        in_specs=[hbm] * 7,
        scratch_shapes=[
            pltpu.VMEM((TOK, LANES), BF16),
            pltpu.VMEM((1, TOK), jnp.int32),
            pltpu.VMEM((1, TOK), jnp.int32),
            pltpu.VMEM((256, LANES), BF16),
            pltpu.VMEM((1, LANES), F32),
            pltpu.VMEM((1, LANES), F32),
            pltpu.VMEM((1, LANES), F32),
            pltpu.SemaphoreType.DMA((7,)),
        ],
        compiler_params=params(60),
    )(
        tile_rows,
        tile_order.reshape(1, TOK),
        tissue_mask.reshape(1, TOK),
        conv_weight.reshape(256, LANES),
        norm_gain.reshape(1, LANES),
        norm_bias.reshape(1, LANES),
        conv_bias.reshape(1, LANES),
    )
    arrived = lax.all_to_all(sorted_rows, "z", split_axis=0, concat_axis=0, tiled=True)
    features = lax.all_gather(wide, "head", axis=0)
    queries = pl.pallas_call(
        query_kernel, out_shape=shape((TOK, LANES), BF16), compiler_params=params(16)
    )(features, query_weight)
    arrived, most, queries = lax.optimization_barrier((arrived, most, queries))
    weights = lax.all_gather(most, "z", axis=0)
    spread = pl.pallas_call(
        spread_kernel,
        out_shape=shape((PLANE, HERE, LANES), BF16),
        out_specs=hbm,
        scratch_shapes=[pltpu.VMEM((HERE, LANES), BF16), pltpu.SemaphoreType.DMA((PLANE,))],
        compiler_params=params(52),
    )(arrived)
    tiles = lax.all_to_all(spread, ("x", "core"), split_axis=0, concat_axis=0, tiled=True)
    tail = arrived[:, ROWS:]
    patches = pl.pallas_call(
        place_kernel,
        out_shape=shape((PATCH, 64, LANES), BF16),
        scratch_shapes=[pltpu.VMEM((PATCH, 64, LANES), F32)],
        compiler_params=params(24),
    )(tiles, weights)
    partial = pl.pallas_call(
        conv_kernel,
        out_shape=shape((NX, NC, NH, 16, LANES), F32),
        compiler_params=params(16),
    )(patches, weights, tail)
    sums = lax.all_to_all(
        partial.reshape(PLANE * NH, 16, LANES),
        ("x", "core", "head"),
        split_axis=0,
        concat_axis=0,
        tiled=True,
    )
    key_value = pl.pallas_call(
        norm_kernel, out_shape=shape((NZ, 32, 256), BF16), compiler_params=params(16)
    )(sums.reshape(NX, NC, NH, 16, LANES), features, key_weight, value_weight)
    gathered = lax.all_to_all(key_value, "z", split_axis=0, concat_axis=0, tiled=True)
    gathered = lax.all_gather(gathered.reshape(NZ * 32, 256), "core", axis=0, tiled=True)
    parts = pl.pallas_call(
        attend_kernel, out_shape=shape((NH, TOK, LANES), BF16), compiler_params=params(24)
    )(queries, gathered, out_weight, tissue_mask.reshape(1, TOK))
    parts = lax.all_to_all(parts, "head", split_axis=0, concat_axis=0, tiled=True)
    return jnp.sum(parts.astype(F32), 0).astype(BF16)


def solution(mesh):
    grid = Mesh(mesh.devices.reshape(NX, NZ, NC, NH), ("x", "z", "core", "head"))
    seq = ("x", "z", "core")
    return jax.shard_map(
        local,
        mesh=grid,
        in_specs=(
            P(seq, "head"),
            P(seq),
            P(seq),
            P(seq, None, "head"),
            P("head"),
            P("head"),
            P("head"),
            P(None, "head"),
            P(None, "head"),
            P(None, "head"),
            P("head", None),
        ),
        out_specs=P(seq, "head"),
        check_vma=False,
    )
```

```python
import math

import jax
import jax.numpy as jnp
from jax import lax
from jax.experimental import pallas as pl
from jax.experimental.pallas import tpu as pltpu
from jax.sharding import Mesh
from jax.sharding import PartitionSpec as P

NX, NZ, NC, NH = 4, 16, 2, 4
PLANE = NX * NC
SLOTS = 8
ROWS = PLANE * SLOTS
SEND = ROWS + 8
TOK = 512
MOST = 252
WIDE = TOK + 48
LANES = 128
BLK = 8
PATCH = 64
EMPTY = 1024.0
HERE = PLANE * 128 + 16
F32 = jnp.float32
BF16 = jnp.bfloat16
NT = (((1,), (1,)), ((), ()))
TN = (((0,), (0,)), ((), ()))


def params(mib):
    return pltpu.CompilerParams(vmem_limit_bytes=mib * 1024 * 1024)


def iota(shape, dim):
    return lax.broadcasted_iota(jnp.int32, shape, dim)


def route_kernel(
    rows_hbm, order_hbm, mask_hbm, kernel_hbm, gain_hbm, shift_hbm, bias_hbm,
    out_ref, wide_ref, most_ref,
    rows_ref, order_ref, mask_ref, kernel_ref, gain_ref, shift_ref, bias_ref, sems,
):
    pairs = (
        (order_hbm, order_ref),
        (mask_hbm, mask_ref),
        (rows_hbm, rows_ref),
        (kernel_hbm, kernel_ref),
        (gain_hbm, gain_ref),
        (shift_hbm, shift_ref),
        (bias_hbm, bias_ref),
    )
    copies = [
        pltpu.make_async_copy(source, held, sems.at[index])
        for index, (source, held) in enumerate(pairs)
    ]
    for copy in copies:
        copy.start()
    before = jnp.where(iota((TOK, TOK), 0) < iota((TOK, TOK), 1), 1.0, 0.0).astype(BF16)
    row256, lane256 = iota((256, 256), 0), iota((256, 256), 1)
    turn = jnp.where(lane256 == (row256 & 3) * PATCH + (row256 >> 2), 1.0, 0.0).astype(BF16)
    for copy in copies:
        copy.wait()
    wide_ref[0:TOK, :] = rows_ref[...]
    whole = jnp.concatenate(
        [gain_ref[...], shift_ref[...], bias_ref[...], jnp.zeros((13, LANES), F32)], 0
    )
    high = whole.astype(BF16)
    rest = whole - high.astype(F32)
    middle = rest.astype(BF16)
    low = (rest - middle.astype(F32)).astype(BF16)
    wide_ref[TOK : TOK + 16, :] = high
    wide_ref[TOK + 16 : TOK + 32, :] = middle
    wide_ref[TOK + 32 : WIDE, :] = low
    turned = jnp.dot(turn, kernel_ref[...], preferred_element_type=F32)
    most_ref[...] = turned[0:MOST, :].astype(BF16)
    tail = turned[MOST - 4 : 256, :]
    lower = iota((8, LANES), 0) < 4
    order = order_ref[...]
    row, col = order >> 9, order & 511
    owner = (row >> 3) * 8 + (col >> 6)
    plane = (owner >> 1) & 15
    place = (owner >> 5) * 2 + (owner & 1)
    target = ((row & 7) * 8 + (col & 7)) * BLK + ((col >> 3) & 7)
    code = plane * PLANE + place
    onehot = jnp.where(iota((128, TOK), 0) == code, 1.0, 0.0)
    counts = jnp.dot(onehot.astype(BF16), before, preferred_element_type=F32)
    rank = jnp.sum(onehot * counts, 0, keepdims=True).astype(jnp.int32)
    slot = place * SLOTS + rank
    here = iota((NZ, TOK), 0) == plane
    value = jnp.where(here, (target - 256).astype(F32), 0.0).astype(BF16)
    there = jnp.where(here, 1.0, 0.0).astype(BF16)
    lane_of = jnp.where(iota((LANES, TOK), 0) == slot, 1.0, 0.0).astype(BF16)
    values = lax.dot_general(value, lane_of, NT, preferred_element_type=F32)
    valid = lax.dot_general(there, lane_of, NT, preferred_element_type=F32)
    meta = jnp.where(valid > 0.5, values, EMPTY)
    wanted = jnp.where(mask_ref[...] != 0, plane * ROWS + slot, -1)
    rows = rows_ref[...]
    for z in range(NZ):
        pick = jnp.where(iota((ROWS, TOK), 0) + z * ROWS == wanted, 1.0, 0.0).astype(BF16)
        out_ref[z, 0:ROWS, :] = jnp.dot(pick, rows, preferred_element_type=F32).astype(BF16)
        last = jnp.where(lower, jnp.broadcast_to(meta[z : z + 1, :], (8, LANES)), tail)
        out_ref[z, ROWS:SEND, :] = last.astype(BF16)


def spread_kernel(arrived_ref, out_hbm, here_ref, sems):
    for owner in range(PLANE):
        rows = arrived_ref[:, owner * SLOTS : owner * SLOTS + SLOTS, :]
        here_ref[owner * 128 : owner * 128 + 128, :] = rows.reshape(128, LANES)
    last = arrived_ref[:, ROWS:SEND, :].astype(F32)
    rows = jnp.concatenate([last[z, 0:1, :] for z in range(NZ)], 0).astype(BF16)
    source, lane = iota((LANES, LANES), 0), iota((LANES, LANES), 1)
    own = iota((NZ, LANES), 0) == (iota((NZ, LANES), 1) >> 3)
    found = []
    for owner in range(PLANE):
        pick = jnp.where(source == owner * SLOTS + (lane & 7), 1.0, 0.0).astype(BF16)
        moved = jnp.dot(rows, pick, preferred_element_type=F32)
        found.append(jnp.sum(jnp.where(own, moved, 0.0), 0, keepdims=True))
    found.append(jnp.zeros((8, LANES), F32))
    here_ref[PLANE * 128 : HERE, :] = jnp.concatenate(found, 0).astype(BF16)
    copies = [
        pltpu.make_async_copy(here_ref, out_hbm.at[index], sems.at[index])
        for index in range(PLANE)
    ]
    for copy in copies:
        copy.start()
    for copy in copies:
        copy.wait()


def place_kernel(tile_ref, weight_ref, out_ref, patch_ref):
    half = TOK // 2
    spot = (iota((half, LANES), 0) - half).astype(F32)
    eye = jnp.where(iota((LANES, LANES), 0) == iota((LANES, LANES), 1), 1.0, 0.0).astype(BF16)
    metas, highs = [], []
    for source in range(PLANE):
        places = tile_ref[source, PLANE * 128 : HERE, :].astype(F32)
        high = jnp.where(places >= 0, 1.0, 0.0)
        metas.append(places - half * high)
        highs.append(lax.dot_general(eye, high.astype(BF16), NT, preferred_element_type=F32))
    for owner in range(PLANE):
        picks, tiles = [], []
        for source in range(PLANE):
            meta = metas[source][owner : owner + 1, :]
            picks.append(jnp.where(spot == meta, 1.0, 0.0).astype(BF16))
            rows = tile_ref[source, owner * 128 : owner * 128 + 128, :]
            upper = rows * highs[source][:, owner : owner + 1].astype(BF16)
            tiles.append(jnp.concatenate([rows - upper, upper], 1))
        total = jnp.dot(
            jnp.concatenate(picks, 1), jnp.concatenate(tiles, 0), preferred_element_type=F32
        )
        at = slice(owner * BLK, owner * BLK + BLK)
        patch_ref[0:32, at, :] = total[:, 0:LANES].reshape(32, BLK, LANES)
        patch_ref[32:PATCH, at, :] = total[:, LANES:].reshape(32, BLK, LANES)
    out_ref[...] = patch_ref[...].astype(BF16)


def conv_kernel(patch_ref, weight_ref, tail_ref, out_ref):
    acc = jnp.zeros((256, 256), F32)
    for quad in range(16):
        if quad < 15:
            left = weight_ref[:, quad * 16 : quad * 16 + 16, :]
        else:
            most = weight_ref[:, quad * 16 : MOST, :].astype(F32)
            left = jnp.concatenate([most, tail_ref[:, 4:8, :].astype(F32)], 1).astype(BF16)
        left = left.reshape(256, LANES)
        right = patch_ref[quad * 4 : quad * 4 + 4, :, :].reshape(256, LANES)
        acc = acc + lax.dot_general(right, left, NT, preferred_element_type=F32)
    column = iota((64, 256), 1)
    kept = jnp.zeros((64, 256), F32)
    for step in range(4):
        kept = kept + jnp.where(
            ((column >> 2) & 3) == step, acc[step * 64 : step * 64 + 64, :], 0.0
        )
    source, lane = iota((256, LANES), 0), iota((256, LANES), 1)
    from_lane = (source >> 4) * 4 + (source & 3)
    lower = jnp.where(from_lane == lane, 1.0, 0.0)
    upper = jnp.where(from_lane + 64 == lane, 1.0, 0.0)

    def merge(rows, hits):
        return jnp.dot(rows, hits, precision=lax.Precision.HIGHEST, preferred_element_type=F32)

    low = merge(kept[0:32], lower).reshape(2, NC, BLK, LANES)
    high = merge(kept[32:64], upper).reshape(2, NC, BLK, LANES)
    for c in range(NC):
        sent = (low[:, c] + high[:, c]).reshape(16, LANES)
        for x in range(NX):
            for head in range(NH):
                out_ref[x, c, head] = sent


def norm_kernel(sums_ref, wide_ref, key_ref, value_ref, out_ref):
    count = 32
    left = iota((count, LANES), 1) < 64
    source, lane = iota((LANES, LANES), 0), iota((LANES, LANES), 1)
    hits = [(lane == (source >> 2) * 8 + c * 4 + (source & 3)) & (source < 64) for c in range(NC)]
    backs = [(source == (lane >> 2) * 8 + c * 4 + (lane & 3)) & (lane < 64) for c in range(NC)]
    shares, gains, biases = [], [], []
    for x in range(NX):
        whole = (
            wide_ref[x, TOK : TOK + 16, :].astype(F32)
            + wide_ref[x, TOK + 16 : TOK + 32, :].astype(F32)
        ) + wide_ref[x, TOK + 32 : WIDE, :].astype(F32)
        for c in range(NC):
            total = sums_ref[x, c, 0]
            for head in range(1, NH):
                total = total + sums_ref[x, c, head]
            total = jnp.concatenate([total, pltpu.roll(total, 64, 1)], 0)
            extra = jnp.dot(
                whole,
                jnp.where(backs[c], 1.0, 0.0),
                precision=lax.Precision.HIGHEST,
                preferred_element_type=F32,
            )
            gains.append(extra[0:1, :])
            biases.append(extra[1:2, :])
            shares.append(jnp.where(left, total + extra[2:3, :], 0.0))
    first = shares[0]
    second = shares[0] * shares[0]
    for share in shares[1:]:
        first = first + share
        second = second + share * share
    center = jnp.sum(first, 1, keepdims=True) * (1.0 / 512)
    spread = jnp.sum(second, 1, keepdims=True) * (1.0 / 512)
    scale = lax.rsqrt(spread - center * center + 1e-05)
    keys = jnp.zeros((count, LANES), F32)
    values = jnp.zeros((count, LANES), F32)
    for x in range(NX):
        natural = None
        for c in range(NC):
            index = x * NC + c
            normed = (shares[index] - center) * scale * gains[index] + biases[index]
            normed = jnp.where(left, normed, 0.0).astype(BF16)
            part = jnp.dot(
                normed, jnp.where(hits[c], 1.0, 0.0).astype(BF16), preferred_element_type=F32
            )
            natural = part if natural is None else natural + part
        natural = natural.astype(BF16)
        keys = keys + jnp.dot(
            natural, key_ref[x * 128 : x * 128 + 128, :], preferred_element_type=F32
        )
        values = values + jnp.dot(
            natural, value_ref[x * 128 : x * 128 + 128, :], preferred_element_type=F32
        )
    both = jnp.concatenate([keys, values], 1).astype(BF16)
    for z in range(NZ):
        out_ref[z] = both


def query_kernel(features_ref, weight_ref, out_ref):
    total = None
    for head in range(NH):
        part = jnp.dot(
            features_ref[head, 0:TOK, :],
            weight_ref[head * 128 : head * 128 + 128, :],
            preferred_element_type=F32,
        )
        total = part if total is None else total + part
    out_ref[...] = total.astype(BF16)


def attend_kernel(query_ref, key_value_ref, weight_ref, mask_ref, out_ref):
    factor = math.log2(math.e) / math.sqrt(64)
    keys = key_value_ref[:, 0:128]
    values = key_value_ref[:, 128:256]
    query = query_ref[...]
    lane, row = iota((TOK, LANES), 1), iota((LANES, TOK), 0)
    mixed = []
    for head in range(2):
        masked = jnp.where((lane >> 6) == head, query.astype(F32), 0.0).astype(BF16)
        scores = lax.dot_general(keys, masked, NT, preferred_element_type=F32)
        highest = jnp.max(scores, 0, keepdims=True)
        weights = jnp.exp2((scores - highest) * factor)
        totals = jnp.sum(weights, 0, keepdims=True)
        mix = lax.dot_general(values, weights.astype(BF16), TN, preferred_element_type=F32)
        mixed.append(mix / totals)
    attended = jnp.where(row < 64, mixed[0], mixed[1])
    attended = jnp.where(mask_ref[...] != 0, attended, 0.0).astype(BF16)
    part = lax.dot_general(attended, weight_ref[...], TN, preferred_element_type=F32).astype(BF16)
    for group in range(NH):
        out_ref[group] = part[:, group * 128 : group * 128 + 128]


def local(
    tile_rows,
    tile_order,
    tissue_mask,
    conv_weight,
    conv_bias,
    norm_gain,
    norm_bias,
    query_weight,
    key_weight,
    value_weight,
    out_weight,
):
    shape = jax.ShapeDtypeStruct
    hbm = pl.BlockSpec(memory_space=pl.ANY)
    sorted_rows, wide, most = pl.pallas_call(
        route_kernel,
        out_shape=(
            shape((NZ, SEND, LANES), BF16),
            shape((WIDE, LANES), BF16),
            shape((MOST, LANES), BF16),
        ),
        in_specs=[hbm] * 7,
        scratch_shapes=[
            pltpu.VMEM((TOK, LANES), BF16),
            pltpu.VMEM((1, TOK), jnp.int32),
            pltpu.VMEM((1, TOK), jnp.int32),
            pltpu.VMEM((256, LANES), BF16),
            pltpu.VMEM((1, LANES), F32),
            pltpu.VMEM((1, LANES), F32),
            pltpu.VMEM((1, LANES), F32),
            pltpu.SemaphoreType.DMA((7,)),
        ],
        compiler_params=params(60),
    )(
        tile_rows,
        tile_order.reshape(1, TOK),
        tissue_mask.reshape(1, TOK),
        conv_weight.reshape(256, LANES),
        norm_gain.reshape(1, LANES),
        norm_bias.reshape(1, LANES),
        conv_bias.reshape(1, LANES),
    )
    arrived = lax.all_to_all(sorted_rows, "z", split_axis=0, concat_axis=0, tiled=True)
    features = lax.all_gather(wide, "head", axis=0)
    queries = pl.pallas_call(
        query_kernel, out_shape=shape((TOK, LANES), BF16), compiler_params=params(16)
    )(features, query_weight)
    arrived, most, queries = lax.optimization_barrier((arrived, most, queries))
    weights = lax.all_gather(most, "z", axis=0)
    spread = pl.pallas_call(
        spread_kernel,
        out_shape=shape((PLANE, HERE, LANES), BF16),
        out_specs=hbm,
        scratch_shapes=[pltpu.VMEM((HERE, LANES), BF16), pltpu.SemaphoreType.DMA((PLANE,))],
        compiler_params=params(52),
    )(arrived)
    tiles = lax.all_to_all(spread, ("x", "core"), split_axis=0, concat_axis=0, tiled=True)
    tail = arrived[:, ROWS:]
    patches = pl.pallas_call(
        place_kernel,
        out_shape=shape((PATCH, 64, LANES), BF16),
        scratch_shapes=[pltpu.VMEM((PATCH, 64, LANES), F32)],
        compiler_params=params(24),
    )(tiles, weights)
    partial = pl.pallas_call(
        conv_kernel,
        out_shape=shape((NX, NC, NH, 16, LANES), F32),
        compiler_params=params(16),
    )(patches, weights, tail)
    sums = lax.all_to_all(
        partial.reshape(PLANE * NH, 16, LANES),
        ("x", "core", "head"),
        split_axis=0,
        concat_axis=0,
        tiled=True,
    )
    key_value = pl.pallas_call(
        norm_kernel, out_shape=shape((NZ, 32, 256), BF16), compiler_params=params(16)
    )(sums.reshape(NX, NC, NH, 16, LANES), features, key_weight, value_weight)
    gathered = lax.all_to_all(key_value, "z", split_axis=0, concat_axis=0, tiled=True)
    gathered = lax.all_gather(gathered.reshape(NZ * 32, 256), "core", axis=0, tiled=True)
    parts = pl.pallas_call(
        attend_kernel, out_shape=shape((NH, TOK, LANES), BF16), compiler_params=params(24)
    )(queries, gathered, out_weight, tissue_mask.reshape(1, TOK))
    parts = lax.all_to_all(parts, "head", split_axis=0, concat_axis=0, tiled=True)
    return jnp.sum(parts.astype(F32), 0).astype(BF16)


def solution(mesh):
    grid = Mesh(mesh.devices.reshape(NX, NZ, NC, NH), ("x", "z", "core", "head"))
    seq = ("x", "z", "core")
    return jax.shard_map(
        local,
        mesh=grid,
        in_specs=(
            P(seq, "head"),
            P(seq),
            P(seq),
            P(seq, None, "head"),
            P("head"),
            P("head"),
            P("head"),
            P(None, "head"),
            P(None, "head"),
            P(None, "head"),
            P("head", None),
        ),
        out_specs=P(seq, "head"),
        check_vma=False,
    )
```

```python
import math

import jax
import jax.numpy as jnp
from jax import lax
from jax.experimental import pallas as pl
from jax.experimental.pallas import tpu as pltpu
from jax.sharding import Mesh
from jax.sharding import PartitionSpec as P

NX, NZ, NC, NH = 4, 16, 2, 4
PLANE = NX * NC
SLOTS = 8
ROWS = PLANE * SLOTS
SEND = ROWS + 8
TOK = 512
MOST = 252
WIDE = TOK + 48
LANES = 128
BLK = 8
PATCH = 64
EMPTY = 1024.0
HERE = PLANE * 128 + 16
F32 = jnp.float32
BF16 = jnp.bfloat16
NT = (((1,), (1,)), ((), ()))
TN = (((0,), (0,)), ((), ()))


def params(mib):
    return pltpu.CompilerParams(vmem_limit_bytes=mib * 1024 * 1024)


def iota(shape, dim):
    return lax.broadcasted_iota(jnp.int32, shape, dim)


def route_kernel(
    rows_hbm, order_hbm, mask_hbm, kernel_hbm, gain_hbm, shift_hbm, bias_hbm,
    out_ref, wide_ref, most_ref,
    rows_ref, order_ref, mask_ref, kernel_ref, gain_ref, shift_ref, bias_ref, sems,
):
    pairs = (
        (order_hbm, order_ref),
        (mask_hbm, mask_ref),
        (rows_hbm, rows_ref),
        (kernel_hbm, kernel_ref),
        (gain_hbm, gain_ref),
        (shift_hbm, shift_ref),
        (bias_hbm, bias_ref),
    )
    copies = [
        pltpu.make_async_copy(source, held, sems.at[index])
        for index, (source, held) in enumerate(pairs)
    ]
    for copy in copies:
        copy.start()
    before = jnp.where(iota((TOK, TOK), 0) < iota((TOK, TOK), 1), 1.0, 0.0).astype(BF16)
    row256, lane256 = iota((256, 256), 0), iota((256, 256), 1)
    turn = jnp.where(lane256 == (row256 & 3) * PATCH + (row256 >> 2), 1.0, 0.0).astype(BF16)
    for copy in copies:
        copy.wait()
    wide_ref[0:TOK, :] = rows_ref[...]
    whole = jnp.concatenate(
        [gain_ref[...], shift_ref[...], bias_ref[...], jnp.zeros((13, LANES), F32)], 0
    )
    high = whole.astype(BF16)
    rest = whole - high.astype(F32)
    middle = rest.astype(BF16)
    low = (rest - middle.astype(F32)).astype(BF16)
    wide_ref[TOK : TOK + 16, :] = high
    wide_ref[TOK + 16 : TOK + 32, :] = middle
    wide_ref[TOK + 32 : WIDE, :] = low
    turned = jnp.dot(turn, kernel_ref[...], preferred_element_type=F32)
    most_ref[...] = turned[0:MOST, :].astype(BF16)
    tail = turned[MOST - 4 : 256, :]
    lower = iota((8, LANES), 0) < 4
    order = order_ref[...]
    row, col = order >> 9, order & 511
    owner = (row >> 3) * 8 + (col >> 6)
    plane = (owner >> 1) & 15
    place = (owner >> 5) * 2 + (owner & 1)
    target = ((row & 7) * 8 + (col & 7)) * BLK + ((col >> 3) & 7)
    code = plane * PLANE + place
    onehot = jnp.where(iota((128, TOK), 0) == code, 1.0, 0.0)
    counts = jnp.dot(onehot.astype(BF16), before, preferred_element_type=F32)
    rank = jnp.sum(onehot * counts, 0, keepdims=True).astype(jnp.int32)
    slot = place * SLOTS + rank
    here = iota((NZ, TOK), 0) == plane
    value = jnp.where(here, (target - 256).astype(F32), 0.0).astype(BF16)
    there = jnp.where(here, 1.0, 0.0).astype(BF16)
    lane_of = jnp.where(iota((LANES, TOK), 0) == slot, 1.0, 0.0).astype(BF16)
    values = lax.dot_general(value, lane_of, NT, preferred_element_type=F32)
    valid = lax.dot_general(there, lane_of, NT, preferred_element_type=F32)
    meta = jnp.where(valid > 0.5, values, EMPTY)
    wanted = jnp.where(mask_ref[...] != 0, plane * ROWS + slot, -1)
    rows = rows_ref[...]
    for z in range(NZ):
        pick = jnp.where(iota((ROWS, TOK), 0) + z * ROWS == wanted, 1.0, 0.0).astype(BF16)
        out_ref[z, 0:ROWS, :] = jnp.dot(pick, rows, preferred_element_type=F32).astype(BF16)
        last = jnp.where(lower, jnp.broadcast_to(meta[z : z + 1, :], (8, LANES)), tail)
        out_ref[z, ROWS:SEND, :] = last.astype(BF16)


def spread_kernel(arrived_ref, out_hbm, here_ref, sems):
    for owner in range(PLANE):
        rows = arrived_ref[:, owner * SLOTS : owner * SLOTS + SLOTS, :]
        here_ref[owner * 128 : owner * 128 + 128, :] = rows.reshape(128, LANES)
    last = arrived_ref[:, ROWS:SEND, :].astype(F32)
    rows = jnp.concatenate([last[z, 0:1, :] for z in range(NZ)], 0).astype(BF16)
    source, lane = iota((LANES, LANES), 0), iota((LANES, LANES), 1)
    own = iota((NZ, LANES), 0) == (iota((NZ, LANES), 1) >> 3)
    found = []
    for owner in range(PLANE):
        pick = jnp.where(source == owner * SLOTS + (lane & 7), 1.0, 0.0).astype(BF16)
        moved = jnp.dot(rows, pick, preferred_element_type=F32)
        found.append(jnp.sum(jnp.where(own, moved, 0.0), 0, keepdims=True))
    found.append(jnp.zeros((8, LANES), F32))
    here_ref[PLANE * 128 : HERE, :] = jnp.concatenate(found, 0).astype(BF16)
    copies = [
        pltpu.make_async_copy(here_ref, out_hbm.at[index], sems.at[index])
        for index in range(PLANE)
    ]
    for copy in copies:
        copy.start()
    for copy in copies:
        copy.wait()


def place_kernel(tile_ref, weight_ref, out_ref, patch_ref):
    half = TOK // 2
    spot = (iota((half, LANES), 0) - half).astype(F32)
    eye = jnp.where(iota((LANES, LANES), 0) == iota((LANES, LANES), 1), 1.0, 0.0).astype(BF16)
    metas, highs = [], []
    for source in range(PLANE):
        places = tile_ref[source, PLANE * 128 : HERE, :].astype(F32)
        high = jnp.where(places >= 0, 1.0, 0.0)
        metas.append(places - half * high)
        highs.append(lax.dot_general(eye, high.astype(BF16), NT, preferred_element_type=F32))
    for owner in range(PLANE):
        picks, tiles = [], []
        for source in range(PLANE):
            meta = metas[source][owner : owner + 1, :]
            picks.append(jnp.where(spot == meta, 1.0, 0.0).astype(BF16))
            rows = tile_ref[source, owner * 128 : owner * 128 + 128, :]
            upper = rows * highs[source][:, owner : owner + 1].astype(BF16)
            tiles.append(jnp.concatenate([rows - upper, upper], 1))
        total = jnp.dot(
            jnp.concatenate(picks, 1), jnp.concatenate(tiles, 0), preferred_element_type=F32
        )
        at = slice(owner * BLK, owner * BLK + BLK)
        patch_ref[0:32, at, :] = total[:, 0:LANES].reshape(32, BLK, LANES)
        patch_ref[32:PATCH, at, :] = total[:, LANES:].reshape(32, BLK, LANES)
    out_ref[...] = patch_ref[...].astype(BF16)


def conv_kernel(patch_ref, weight_ref, tail_ref, out_ref):
    acc = jnp.zeros((256, 256), F32)
    for quad in range(16):
        if quad < 15:
            left = weight_ref[:, quad * 16 : quad * 16 + 16, :]
        else:
            most = weight_ref[:, quad * 16 : MOST, :].astype(F32)
            left = jnp.concatenate([most, tail_ref[:, 4:8, :].astype(F32)], 1).astype(BF16)
        left = left.reshape(256, LANES)
        right = patch_ref[quad * 4 : quad * 4 + 4, :, :].reshape(256, LANES)
        acc = acc + lax.dot_general(right, left, NT, preferred_element_type=F32)
    column = iota((64, 256), 1)
    kept = jnp.zeros((64, 256), F32)
    for step in range(4):
        kept = kept + jnp.where(
            ((column >> 2) & 3) == step, acc[step * 64 : step * 64 + 64, :], 0.0
        )
    source, lane = iota((256, LANES), 0), iota((256, LANES), 1)
    from_lane = (source >> 4) * 4 + (source & 3)
    lower = jnp.where(from_lane == lane, 1.0, 0.0)
    upper = jnp.where(from_lane + 64 == lane, 1.0, 0.0)

    def merge(rows, hits):
        return jnp.dot(rows, hits, precision=lax.Precision.HIGHEST, preferred_element_type=F32)

    low = merge(kept[0:32], lower).reshape(2, NC, BLK, LANES)
    high = merge(kept[32:64], upper).reshape(2, NC, BLK, LANES)
    for c in range(NC):
        sent = (low[:, c] + high[:, c]).reshape(16, LANES)
        for x in range(NX):
            for head in range(NH):
                out_ref[x, c, head] = sent


def norm_kernel(sums_ref, extra_ref, key_ref, value_ref, out_ref):
    count = 32
    left = iota((count, LANES), 1) < 64
    source, lane = iota((LANES, LANES), 0), iota((LANES, LANES), 1)
    hits = [(lane == (source >> 2) * 8 + c * 4 + (source & 3)) & (source < 64) for c in range(NC)]
    shares, gains, biases = [], [], []
    for x in range(NX):
        for c in range(NC):
            total = sums_ref[x, c, 0]
            for head in range(1, NH):
                total = total + sums_ref[x, c, head]
            total = jnp.concatenate([total, pltpu.roll(total, 64, 1)], 0)
            extra = extra_ref[x * NC + c]
            gains.append(extra[0:1, :])
            biases.append(extra[1:2, :])
            shares.append(jnp.where(left, total + extra[2:3, :], 0.0))
    first = shares[0]
    second = shares[0] * shares[0]
    for share in shares[1:]:
        first = first + share
        second = second + share * share
    center = jnp.sum(first, 1, keepdims=True) * (1.0 / 512)
    spread = jnp.sum(second, 1, keepdims=True) * (1.0 / 512)
    scale = lax.rsqrt(spread - center * center + 1e-05)
    keys = jnp.zeros((count, LANES), F32)
    values = jnp.zeros((count, LANES), F32)
    for x in range(NX):
        natural = None
        for c in range(NC):
            index = x * NC + c
            normed = (shares[index] - center) * scale * gains[index] + biases[index]
            normed = jnp.where(left, normed, 0.0).astype(BF16)
            part = jnp.dot(
                normed, jnp.where(hits[c], 1.0, 0.0).astype(BF16), preferred_element_type=F32
            )
            natural = part if natural is None else natural + part
        natural = natural.astype(BF16)
        keys = keys + jnp.dot(
            natural, key_ref[x * 128 : x * 128 + 128, :], preferred_element_type=F32
        )
        values = values + jnp.dot(
            natural, value_ref[x * 128 : x * 128 + 128, :], preferred_element_type=F32
        )
    both = jnp.concatenate([keys, values], 1).astype(BF16)
    for z in range(NZ):
        out_ref[z] = both


def query_kernel(features_ref, weight_ref, out_ref, extra_ref):
    total = None
    for head in range(NH):
        part = jnp.dot(
            features_ref[head, 0:TOK, :],
            weight_ref[head * 128 : head * 128 + 128, :],
            preferred_element_type=F32,
        )
        total = part if total is None else total + part
    out_ref[...] = total.astype(BF16)
    source, lane = iota((LANES, LANES), 0), iota((LANES, LANES), 1)
    for x in range(NX):
        whole = (
            features_ref[x, TOK : TOK + 16, :].astype(F32)
            + features_ref[x, TOK + 16 : TOK + 32, :].astype(F32)
        ) + features_ref[x, TOK + 32 : WIDE, :].astype(F32)
        for c in range(NC):
            back = (source == (lane >> 2) * 8 + c * 4 + (lane & 3)) & (lane < 64)
            extra = jnp.dot(
                whole,
                jnp.where(back, 1.0, 0.0),
                precision=lax.Precision.HIGHEST,
                preferred_element_type=F32,
            )
            extra_ref[x * NC + c] = extra[0:8, :]


def attend_kernel(query_ref, key_value_ref, weight_ref, mask_ref, out_ref):
    factor = math.log2(math.e) / math.sqrt(64)
    keys = key_value_ref[:, 0:128]
    values = key_value_ref[:, 128:256]
    query = query_ref[...]
    lane, row = iota((TOK, LANES), 1), iota((LANES, TOK), 0)
    mixed = []
    for head in range(2):
        masked = jnp.where((lane >> 6) == head, query.astype(F32), 0.0).astype(BF16)
        scores = lax.dot_general(keys, masked, NT, preferred_element_type=F32)
        highest = jnp.max(scores, 0, keepdims=True)
        weights = jnp.exp2((scores - highest) * factor)
        totals = jnp.sum(weights, 0, keepdims=True)
        mix = lax.dot_general(values, weights.astype(BF16), TN, preferred_element_type=F32)
        mixed.append(mix / totals)
    attended = jnp.where(row < 64, mixed[0], mixed[1])
    attended = jnp.where(mask_ref[...] != 0, attended, 0.0).astype(BF16)
    part = lax.dot_general(attended, weight_ref[...], TN, preferred_element_type=F32).astype(BF16)
    for group in range(NH):
        out_ref[group] = part[:, group * 128 : group * 128 + 128]


def local(
    tile_rows,
    tile_order,
    tissue_mask,
    conv_weight,
    conv_bias,
    norm_gain,
    norm_bias,
    query_weight,
    key_weight,
    value_weight,
    out_weight,
):
    shape = jax.ShapeDtypeStruct
    hbm = pl.BlockSpec(memory_space=pl.ANY)
    sorted_rows, wide, most = pl.pallas_call(
        route_kernel,
        out_shape=(
            shape((NZ, SEND, LANES), BF16),
            shape((WIDE, LANES), BF16),
            shape((MOST, LANES), BF16),
        ),
        in_specs=[hbm] * 7,
        scratch_shapes=[
            pltpu.VMEM((TOK, LANES), BF16),
            pltpu.VMEM((1, TOK), jnp.int32),
            pltpu.VMEM((1, TOK), jnp.int32),
            pltpu.VMEM((256, LANES), BF16),
            pltpu.VMEM((1, LANES), F32),
            pltpu.VMEM((1, LANES), F32),
            pltpu.VMEM((1, LANES), F32),
            pltpu.SemaphoreType.DMA((7,)),
        ],
        compiler_params=params(60),
    )(
        tile_rows,
        tile_order.reshape(1, TOK),
        tissue_mask.reshape(1, TOK),
        conv_weight.reshape(256, LANES),
        norm_gain.reshape(1, LANES),
        norm_bias.reshape(1, LANES),
        conv_bias.reshape(1, LANES),
    )
    arrived = lax.all_to_all(sorted_rows, "z", split_axis=0, concat_axis=0, tiled=True)
    features = lax.all_gather(wide, "head", axis=0)
    queries, extra = pl.pallas_call(
        query_kernel,
        out_shape=(shape((TOK, LANES), BF16), shape((PLANE, 8, LANES), F32)),
        compiler_params=params(16),
    )(features, query_weight)
    arrived, most, queries = lax.optimization_barrier((arrived, most, queries))
    weights = lax.all_gather(most, "z", axis=0)
    spread = pl.pallas_call(
        spread_kernel,
        out_shape=shape((PLANE, HERE, LANES), BF16),
        out_specs=hbm,
        scratch_shapes=[pltpu.VMEM((HERE, LANES), BF16), pltpu.SemaphoreType.DMA((PLANE,))],
        compiler_params=params(52),
    )(arrived)
    tiles = lax.all_to_all(spread, ("x", "core"), split_axis=0, concat_axis=0, tiled=True)
    tail = arrived[:, ROWS:]
    patches = pl.pallas_call(
        place_kernel,
        out_shape=shape((PATCH, 64, LANES), BF16),
        scratch_shapes=[pltpu.VMEM((PATCH, 64, LANES), F32)],
        compiler_params=params(24),
    )(tiles, weights)
    partial = pl.pallas_call(
        conv_kernel,
        out_shape=shape((NX, NC, NH, 16, LANES), F32),
        compiler_params=params(16),
    )(patches, weights, tail)
    sums = lax.all_to_all(
        partial.reshape(PLANE * NH, 16, LANES),
        ("x", "core", "head"),
        split_axis=0,
        concat_axis=0,
        tiled=True,
    )
    key_value = pl.pallas_call(
        norm_kernel, out_shape=shape((NZ, 32, 256), BF16), compiler_params=params(16)
    )(sums.reshape(NX, NC, NH, 16, LANES), extra, key_weight, value_weight)
    gathered = lax.all_to_all(key_value, "z", split_axis=0, concat_axis=0, tiled=True)
    gathered = lax.all_gather(gathered.reshape(NZ * 32, 256), "core", axis=0, tiled=True)
    parts = pl.pallas_call(
        attend_kernel, out_shape=shape((NH, TOK, LANES), BF16), compiler_params=params(24)
    )(queries, gathered, out_weight, tissue_mask.reshape(1, TOK))
    parts = lax.all_to_all(parts, "head", split_axis=0, concat_axis=0, tiled=True)
    return jnp.sum(parts.astype(F32), 0).astype(BF16)


def solution(mesh):
    grid = Mesh(mesh.devices.reshape(NX, NZ, NC, NH), ("x", "z", "core", "head"))
    seq = ("x", "z", "core")
    return jax.shard_map(
        local,
        mesh=grid,
        in_specs=(
            P(seq, "head"),
            P(seq),
            P(seq),
            P(seq, None, "head"),
            P("head"),
            P("head"),
            P("head"),
            P(None, "head"),
            P(None, "head"),
            P(None, "head"),
            P("head", None),
        ),
        out_specs=P(seq, "head"),
        check_vma=False,
    )
```

```python
import math

import jax
import jax.numpy as jnp
from jax import lax
from jax.experimental import pallas as pl
from jax.experimental.pallas import tpu as pltpu
from jax.sharding import Mesh
from jax.sharding import PartitionSpec as P

NX, NZ, NC, NH = 4, 16, 2, 4
PLANE = NX * NC
SLOTS = 8
ROWS = PLANE * SLOTS
SEND = ROWS + 8
TOK = 512
MOST = 252
WIDE = TOK + 48
LANES = 128
BLK = 8
PATCH = 64
EMPTY = 1024.0
HERE = PLANE * 128 + 16
F32 = jnp.float32
BF16 = jnp.bfloat16
NT = (((1,), (1,)), ((), ()))
TN = (((0,), (0,)), ((), ()))


def params(mib):
    return pltpu.CompilerParams(vmem_limit_bytes=mib * 1024 * 1024)


def iota(shape, dim):
    return lax.broadcasted_iota(jnp.int32, shape, dim)


def route_kernel(
    rows_hbm, order_hbm, mask_hbm, kernel_hbm, gain_hbm, shift_hbm, bias_hbm,
    out_ref, wide_ref, most_ref,
    rows_ref, order_ref, mask_ref, kernel_ref, gain_ref, shift_ref, bias_ref, sems,
):
    pairs = (
        (order_hbm, order_ref),
        (mask_hbm, mask_ref),
        (rows_hbm, rows_ref),
        (kernel_hbm, kernel_ref),
        (gain_hbm, gain_ref),
        (shift_hbm, shift_ref),
        (bias_hbm, bias_ref),
    )
    copies = [
        pltpu.make_async_copy(source, held, sems.at[index])
        for index, (source, held) in enumerate(pairs)
    ]
    for copy in copies:
        copy.start()
    before = jnp.where(iota((TOK, TOK), 0) < iota((TOK, TOK), 1), 1.0, 0.0).astype(BF16)
    row256, lane256 = iota((256, 256), 0), iota((256, 256), 1)
    turn = jnp.where(lane256 == (row256 & 3) * PATCH + (row256 >> 2), 1.0, 0.0).astype(BF16)
    for copy in copies:
        copy.wait()
    wide_ref[0:TOK, :] = rows_ref[...]
    whole = jnp.concatenate(
        [gain_ref[...], shift_ref[...], bias_ref[...], jnp.zeros((13, LANES), F32)], 0
    )
    high = whole.astype(BF16)
    rest = whole - high.astype(F32)
    middle = rest.astype(BF16)
    low = (rest - middle.astype(F32)).astype(BF16)
    wide_ref[TOK : TOK + 16, :] = high
    wide_ref[TOK + 16 : TOK + 32, :] = middle
    wide_ref[TOK + 32 : WIDE, :] = low
    turned = jnp.dot(turn, kernel_ref[...], preferred_element_type=F32)
    most_ref[...] = turned[0:MOST, :].astype(BF16)
    tail = turned[MOST - 4 : 256, :]
    lower = iota((8, LANES), 0) < 4
    order = order_ref[...]
    row, col = order >> 9, order & 511
    owner = (row >> 3) * 8 + (col >> 6)
    plane = (owner >> 1) & 15
    place = (owner >> 5) * 2 + (owner & 1)
    target = ((row & 7) * 8 + (col & 7)) * BLK + ((col >> 3) & 7)
    code = plane * PLANE + place
    onehot = jnp.where(iota((128, TOK), 0) == code, 1.0, 0.0)
    counts = jnp.dot(onehot.astype(BF16), before, preferred_element_type=F32)
    rank = jnp.sum(onehot * counts, 0, keepdims=True).astype(jnp.int32)
    slot = place * SLOTS + rank
    here = iota((NZ, TOK), 0) == plane
    value = jnp.where(here, (target - 256).astype(F32), 0.0).astype(BF16)
    there = jnp.where(here, 1.0, 0.0).astype(BF16)
    lane_of = jnp.where(iota((LANES, TOK), 0) == slot, 1.0, 0.0).astype(BF16)
    values = lax.dot_general(value, lane_of, NT, preferred_element_type=F32)
    valid = lax.dot_general(there, lane_of, NT, preferred_element_type=F32)
    meta = jnp.where(valid > 0.5, values, EMPTY)
    wanted = jnp.where(mask_ref[...] != 0, plane * ROWS + slot, -1)
    rows = rows_ref[...]
    for z in range(NZ):
        pick = jnp.where(iota((ROWS, TOK), 0) + z * ROWS == wanted, 1.0, 0.0).astype(BF16)
        out_ref[z, 0:ROWS, :] = jnp.dot(pick, rows, preferred_element_type=F32).astype(BF16)
        last = jnp.where(lower, jnp.broadcast_to(meta[z : z + 1, :], (8, LANES)), tail)
        out_ref[z, ROWS:SEND, :] = last.astype(BF16)


def spread_kernel(arrived_ref, out_hbm, here_ref, sems):
    for owner in range(PLANE):
        rows = arrived_ref[:, owner * SLOTS : owner * SLOTS + SLOTS, :]
        here_ref[owner * 128 : owner * 128 + 128, :] = rows.reshape(128, LANES)
    last = arrived_ref[:, ROWS:SEND, :].astype(F32)
    rows = jnp.concatenate([last[z, 0:1, :] for z in range(NZ)], 0).astype(BF16)
    source, lane = iota((LANES, LANES), 0), iota((LANES, LANES), 1)
    own = iota((NZ, LANES), 0) == (iota((NZ, LANES), 1) >> 3)
    found = []
    for owner in range(PLANE):
        pick = jnp.where(source == owner * SLOTS + (lane & 7), 1.0, 0.0).astype(BF16)
        moved = jnp.dot(rows, pick, preferred_element_type=F32)
        found.append(jnp.sum(jnp.where(own, moved, 0.0), 0, keepdims=True))
    found.append(jnp.zeros((8, LANES), F32))
    here_ref[PLANE * 128 : HERE, :] = jnp.concatenate(found, 0).astype(BF16)
    copies = [
        pltpu.make_async_copy(here_ref, out_hbm.at[index], sems.at[index])
        for index in range(PLANE)
    ]
    for copy in copies:
        copy.start()
    for copy in copies:
        copy.wait()


def place_kernel(tile_ref, weight_ref, out_ref, patch_ref):
    half = TOK // 2
    spot = (iota((half, LANES), 0) - half).astype(F32)
    eye = jnp.where(iota((LANES, LANES), 0) == iota((LANES, LANES), 1), 1.0, 0.0).astype(BF16)
    metas, highs = [], []
    for source in range(PLANE):
        places = tile_ref[source, PLANE * 128 : HERE, :].astype(F32)
        high = jnp.where(places >= 0, 1.0, 0.0)
        metas.append(places - half * high)
        highs.append(lax.dot_general(eye, high.astype(BF16), NT, preferred_element_type=F32))
    for owner in range(PLANE):
        picks, tiles = [], []
        for source in range(PLANE):
            meta = metas[source][owner : owner + 1, :]
            picks.append(jnp.where(spot == meta, 1.0, 0.0).astype(BF16))
            rows = tile_ref[source, owner * 128 : owner * 128 + 128, :]
            upper = rows * highs[source][:, owner : owner + 1].astype(BF16)
            tiles.append(jnp.concatenate([rows - upper, upper], 1))
        total = jnp.dot(
            jnp.concatenate(picks, 1), jnp.concatenate(tiles, 0), preferred_element_type=F32
        )
        at = slice(owner * BLK, owner * BLK + BLK)
        patch_ref[0:32, at, :] = total[:, 0:LANES].reshape(32, BLK, LANES)
        patch_ref[32:PATCH, at, :] = total[:, LANES:].reshape(32, BLK, LANES)
    out_ref[...] = patch_ref[...].astype(BF16)


def conv_kernel(patch_ref, weight_ref, tail_ref, out_ref):
    acc = jnp.zeros((256, 256), F32)
    for quad in range(16):
        if quad < 15:
            left = weight_ref[:, quad * 16 : quad * 16 + 16, :]
        else:
            most = weight_ref[:, quad * 16 : MOST, :].astype(F32)
            left = jnp.concatenate([most, tail_ref[:, 4:8, :].astype(F32)], 1).astype(BF16)
        left = left.reshape(256, LANES)
        right = patch_ref[quad * 4 : quad * 4 + 4, :, :].reshape(256, LANES)
        acc = acc + lax.dot_general(right, left, NT, preferred_element_type=F32)
    column = iota((64, 256), 1)
    kept = jnp.zeros((64, 256), F32)
    for step in range(4):
        kept = kept + jnp.where(
            ((column >> 2) & 3) == step, acc[step * 64 : step * 64 + 64, :], 0.0
        )
    source, lane = iota((256, LANES), 0), iota((256, LANES), 1)
    from_lane = (source >> 4) * 4 + (source & 3)
    lower = jnp.where(from_lane == lane, 1.0, 0.0)
    upper = jnp.where(from_lane + 64 == lane, 1.0, 0.0)

    def merge(rows, hits):
        return jnp.dot(rows, hits, precision=lax.Precision.HIGHEST, preferred_element_type=F32)

    low = merge(kept[0:32], lower).reshape(2, NC, BLK, LANES)
    high = merge(kept[32:64], upper).reshape(2, NC, BLK, LANES)
    for c in range(NC):
        sent = (low[:, c] + high[:, c]).reshape(16, LANES)
        for x in range(NX):
            for head in range(NH):
                out_ref[x, c, head] = sent


def norm_kernel(sums_ref, extra_ref, key_ref, value_ref, out_ref):
    count = 32
    left = iota((count, LANES), 1) < 64
    source, lane = iota((LANES, LANES), 0), iota((LANES, LANES), 1)
    hits = [(lane == (source >> 2) * 8 + c * 4 + (source & 3)) & (source < 64) for c in range(NC)]
    shares, gains, biases = [], [], []
    for x in range(NX):
        for c in range(NC):
            total = sums_ref[x, c, 0]
            for head in range(1, NH):
                total = total + sums_ref[x, c, head]
            total = jnp.concatenate([total, pltpu.roll(total, 64, 1)], 0)
            extra = extra_ref[x * NC + c]
            gains.append(extra[0:1, :])
            biases.append(extra[1:2, :])
            shares.append(jnp.where(left, total + extra[2:3, :], 0.0))
    first = shares[0]
    second = shares[0] * shares[0]
    for share in shares[1:]:
        first = first + share
        second = second + share * share
    center = jnp.sum(first, 1, keepdims=True) * (1.0 / 512)
    spread = jnp.sum(second, 1, keepdims=True) * (1.0 / 512)
    scale = lax.rsqrt(spread - center * center + 1e-05)
    keys = jnp.zeros((count, LANES), F32)
    values = jnp.zeros((count, LANES), F32)
    for x in range(NX):
        natural = None
        for c in range(NC):
            index = x * NC + c
            normed = (shares[index] - center) * scale * gains[index] + biases[index]
            normed = jnp.where(left, normed, 0.0).astype(BF16)
            part = jnp.dot(
                normed, jnp.where(hits[c], 1.0, 0.0).astype(BF16), preferred_element_type=F32
            )
            natural = part if natural is None else natural + part
        natural = natural.astype(BF16)
        keys = keys + jnp.dot(
            natural, key_ref[x * 128 : x * 128 + 128, :], preferred_element_type=F32
        )
        values = values + jnp.dot(
            natural, value_ref[x * 128 : x * 128 + 128, :], preferred_element_type=F32
        )
    both = jnp.concatenate([keys, values], 1).astype(BF16)
    for z in range(NZ):
        out_ref[z] = both


def query_kernel(features_ref, weight_ref, out_ref, extra_ref):
    total = None
    for head in range(NH):
        part = jnp.dot(
            features_ref[head, 0:TOK, :],
            weight_ref[head * 128 : head * 128 + 128, :],
            preferred_element_type=F32,
        )
        total = part if total is None else total + part
    out_ref[...] = total.astype(BF16)
    source, lane = iota((LANES, LANES), 0), iota((LANES, LANES), 1)
    for x in range(NX):
        whole = (
            features_ref[x, TOK : TOK + 16, :].astype(F32)
            + features_ref[x, TOK + 16 : TOK + 32, :].astype(F32)
        ) + features_ref[x, TOK + 32 : WIDE, :].astype(F32)
        for c in range(NC):
            back = (source == (lane >> 2) * 8 + c * 4 + (lane & 3)) & (lane < 64)
            extra = jnp.dot(
                whole,
                jnp.where(back, 1.0, 0.0),
                precision=lax.Precision.HIGHEST,
                preferred_element_type=F32,
            )
            extra_ref[x * NC + c] = extra[0:8, :]


def attend_kernel(query_ref, key_value_ref, weight_ref, mask_ref, out_ref):
    factor = math.log2(math.e) / math.sqrt(64)
    keys = key_value_ref[:, 0:128]
    values = key_value_ref[:, 128:256]
    query = query_ref[...]
    lane, row = iota((TOK, LANES), 1), iota((LANES, TOK), 0)
    mixed = []
    for head in range(2):
        masked = jnp.where((lane >> 6) == head, query.astype(F32), 0.0).astype(BF16)
        scores = lax.dot_general(keys, masked, NT, preferred_element_type=F32)
        highest = jnp.max(scores, 0, keepdims=True)
        weights = jnp.exp2((scores - highest) * factor)
        totals = jnp.sum(weights, 0, keepdims=True)
        mix = lax.dot_general(values, weights.astype(BF16), TN, preferred_element_type=F32)
        mixed.append(mix * (1.0 / totals))
    attended = jnp.where(row < 64, mixed[0], mixed[1])
    attended = jnp.where(mask_ref[...] != 0, attended, 0.0).astype(BF16)
    part = lax.dot_general(attended, weight_ref[...], TN, preferred_element_type=F32).astype(BF16)
    for group in range(NH):
        out_ref[group] = part[:, group * 128 : group * 128 + 128]


def local(
    tile_rows,
    tile_order,
    tissue_mask,
    conv_weight,
    conv_bias,
    norm_gain,
    norm_bias,
    query_weight,
    key_weight,
    value_weight,
    out_weight,
):
    shape = jax.ShapeDtypeStruct
    hbm = pl.BlockSpec(memory_space=pl.ANY)
    sorted_rows, wide, most = pl.pallas_call(
        route_kernel,
        out_shape=(
            shape((NZ, SEND, LANES), BF16),
            shape((WIDE, LANES), BF16),
            shape((MOST, LANES), BF16),
        ),
        in_specs=[hbm] * 7,
        scratch_shapes=[
            pltpu.VMEM((TOK, LANES), BF16),
            pltpu.VMEM((1, TOK), jnp.int32),
            pltpu.VMEM((1, TOK), jnp.int32),
            pltpu.VMEM((256, LANES), BF16),
            pltpu.VMEM((1, LANES), F32),
            pltpu.VMEM((1, LANES), F32),
            pltpu.VMEM((1, LANES), F32),
            pltpu.SemaphoreType.DMA((7,)),
        ],
        compiler_params=params(60),
    )(
        tile_rows,
        tile_order.reshape(1, TOK),
        tissue_mask.reshape(1, TOK),
        conv_weight.reshape(256, LANES),
        norm_gain.reshape(1, LANES),
        norm_bias.reshape(1, LANES),
        conv_bias.reshape(1, LANES),
    )
    arrived = lax.all_to_all(sorted_rows, "z", split_axis=0, concat_axis=0, tiled=True)
    features = lax.all_gather(wide, "head", axis=0)
    queries, extra = pl.pallas_call(
        query_kernel,
        out_shape=(shape((TOK, LANES), BF16), shape((PLANE, 8, LANES), F32)),
        compiler_params=params(16),
    )(features, query_weight)
    arrived, most, queries = lax.optimization_barrier((arrived, most, queries))
    weights = lax.all_gather(most, "z", axis=0)
    spread = pl.pallas_call(
        spread_kernel,
        out_shape=shape((PLANE, HERE, LANES), BF16),
        out_specs=hbm,
        scratch_shapes=[pltpu.VMEM((HERE, LANES), BF16), pltpu.SemaphoreType.DMA((PLANE,))],
        compiler_params=params(52),
    )(arrived)
    tiles = lax.all_to_all(spread, ("x", "core"), split_axis=0, concat_axis=0, tiled=True)
    tail = arrived[:, ROWS:]
    patches = pl.pallas_call(
        place_kernel,
        out_shape=shape((PATCH, 64, LANES), BF16),
        scratch_shapes=[pltpu.VMEM((PATCH, 64, LANES), F32)],
        compiler_params=params(24),
    )(tiles, weights)
    partial = pl.pallas_call(
        conv_kernel,
        out_shape=shape((NX, NC, NH, 16, LANES), F32),
        compiler_params=params(16),
    )(patches, weights, tail)
    sums = lax.all_to_all(
        partial.reshape(PLANE * NH, 16, LANES),
        ("x", "core", "head"),
        split_axis=0,
        concat_axis=0,
        tiled=True,
    )
    key_value = pl.pallas_call(
        norm_kernel, out_shape=shape((NZ, 32, 256), BF16), compiler_params=params(16)
    )(sums.reshape(NX, NC, NH, 16, LANES), extra, key_weight, value_weight)
    gathered = lax.all_to_all(key_value, "z", split_axis=0, concat_axis=0, tiled=True)
    gathered = lax.all_gather(gathered.reshape(NZ * 32, 256), "core", axis=0, tiled=True)
    parts = pl.pallas_call(
        attend_kernel, out_shape=shape((NH, TOK, LANES), BF16), compiler_params=params(24)
    )(queries, gathered, out_weight, tissue_mask.reshape(1, TOK))
    parts = lax.all_to_all(parts, "head", split_axis=0, concat_axis=0, tiled=True)
    return jnp.sum(parts.astype(F32), 0).astype(BF16)


def solution(mesh):
    grid = Mesh(mesh.devices.reshape(NX, NZ, NC, NH), ("x", "z", "core", "head"))
    seq = ("x", "z", "core")
    return jax.shard_map(
        local,
        mesh=grid,
        in_specs=(
            P(seq, "head"),
            P(seq),
            P(seq),
            P(seq, None, "head"),
            P("head"),
            P("head"),
            P("head"),
            P(None, "head"),
            P(None, "head"),
            P(None, "head"),
            P("head", None),
        ),
        out_specs=P(seq, "head"),
        check_vma=False,
    )
```
